128 devices in a mesh: row: 8 (over x, z_hi), col: 16 (over y, z_lo, core).
Axes of the slice: x: 4, y: 4, z: 4 (z_hi: 2, z_lo: 2; z = z_hi * 2 + z_lo), core: 2. Of those that a mesh axis runs over, the one named last changes fastest.
Arguments:
- a_blocks: bfloat16 [8, 16, 4, 7, 128, 128], P('row', 'col'), may hold values from -6 to 6
- a_rows: int32 [8, 16, 4, 7], P('row', 'col'), may hold values from 0 to 7, as said below
- b_blocks: bfloat16 [8, 16, 2, 4, 3, 128, 128], P('row', 'col'), may hold values from -0.09375 to 0.09375
- b_cols: int32 [8, 16, 2, 4, 3], P('row', 'col'), may hold values from 0 to 3, as said below
- screen: int32 [8, 16, 16, 4, 7, 3], P('row', 'col'), may hold values 0 or 1
- keep: int32 [8, 16, 32], P('row', 'col'), may hold values 0 or 1
- owners: int32 [8, 16, 32, 1], P('row', 'col'), may hold values from 0 to 15; in each aligned block of 32 rows (0 to 31, 32 to 63, ..., all dimensions but the last counted through in order) at most 2 rows name the same one
Outputs:
- owned: bfloat16 [8, 16, 16, 2, 128, 128], P('row', 'col')
The draws below stay inside these ranges and needn't reach their ends.
Inputs may be any that keep to these rules, and one draw needn't show every extreme that they name: `a_rows`: for each device and block column k, the 7 entries are distinct block rows. `b_cols`: for each device, tile and block row k, the 3 entries are distinct block columns. `owners`: among the blocks of one device at most 2 have the same owner.
All inputs are finite; a program needn't handle non-finite values. No bound on the sum of `screen` or of `keep` on one device may be relied on, other than what follows from the above.
Results may differ from the reference program's by a relative error of at most 0.001.
Values may be sent and summed in bfloat16 or wider, within the bound.
A program may use at most 128 MiB of HBM per device.

```python
import math
import jax
import jax.numpy as jnp
import numpy as np
from jax import lax

BS = 128
BK = 4
NA = 7
NBB = 3
SLOT = 2
NB = 64
N_ROW = 8
N_COL = 16


def distinct_lists(key, count, span, taken):
    keys = jax.random.split(key, count)
    return jax.vmap(lambda single: jax.random.permutation(single, span)[:taken])(keys).astype(jnp.int32)


def draw_a_rows(key, part):
    key = jax.random.fold_in(key, 11)
    lists = distinct_lists(key, N_ROW * N_COL * BK, 2 * BK, NA)
    return lists.reshape(N_ROW, N_COL, BK, NA)


def draw_b_cols(key, part):
    key = jax.random.fold_in(key, 23)
    lists = distinct_lists(key, N_ROW * N_COL * 2 * BK, BK, NBB)
    return lists.reshape(N_ROW, N_COL, 2, BK, NBB)


def plant(drawn, stream_key, low, top_value):
    dims = drawn.shape
    spot = [jax.random.randint(jax.random.fold_in(stream_key, axis), (), 0, dims[axis]) for axis in range(len(dims))]
    drawn = drawn.at[tuple(spot)].set(low)
    longest = dims.index(max(dims))
    spot[longest] = (spot[longest] + 1) % dims[longest]
    return drawn.at[tuple(spot)].set(top_value)


def levels(stream_key, dims, cuts, smallest, top_value):
    def one(axis_at, parts):
        steps = jax.random.uniform(jax.random.fold_in(jax.random.fold_in(stream_key, 6), axis_at), (parts,), jnp.float32, smallest / len(cuts), top_value / len(cuts))
        return jnp.repeat(jnp.exp(steps), dims[axis_at] // parts).reshape((-1,) + (1,) * (len(dims) - axis_at - 1))

    factor_of = one(*cuts[0])
    for cut in cuts[1:]:
        factor_of = factor_of * one(*cut)
    return factor_of


def shared_out(stream_key, own, number, rows, count, top, most, slope):
    sequence = jax.random.permutation(stream_key, count)
    crowded, common = portions_of(count, rows * top, most, slope, True), portions_of(count, rows * top, most, slope, False)
    places = jnp.arange(count)

    def named(lengths, turn):
        used = int((lengths > 0).sum())
        fixed = max(1, used // 4)
        moved = fixed + (places - fixed + turn * (used - fixed)) % max(1, count - fixed)
        return jnp.zeros((count,), jnp.int32).at[sequence[jnp.where(places < fixed, places, moved)]].set(jnp.asarray(lengths, jnp.int32))

    lengths = jnp.where(number % 4 == 0, named(crowded, number // 4), named(common, number - number // 4 - 1))
    mixed = jax.random.permutation(jax.random.fold_in(own, 3), count)
    giver, receiver = mixed[0:count // 2 * 2:2], mixed[1:count // 2 * 2:2]
    room = jnp.minimum(lengths[giver] - 1, most - lengths[receiver]) // 2
    room = jnp.where((giver == sequence[0]) | (receiver == sequence[0]) | (lengths[receiver] == 0), 0, jnp.maximum(room, 0))
    moved = jax.random.randint(jax.random.fold_in(own, 4), (count // 2,), 0, 1 << 20) % (room + 1)
    lengths = lengths.at[giver].add(-moved).at[receiver].add(moved)
    members = jnp.searchsorted(jnp.cumsum(lengths), jnp.arange(rows * top), side="right").astype(jnp.int32)
    table = members.reshape(top, rows).T
    table = table[jax.random.permutation(jax.random.fold_in(own, 1), rows)]
    turn = jax.random.randint(jax.random.fold_in(own, 2), (rows, 1), 0, top)
    return jnp.take_along_axis(table, (jnp.arange(top)[None, :] + turn) % top, axis=1)


def portions_of(count, total, limit, skew, full):
    weights = [(1 << 20) // math.isqrt(standing ** skew) + 1 for standing in range(1, count + 1)]
    largest = limit if full else min(limit, max(-(-total // count), total * weights[0] // sum(weights)))
    least = 1 if total - largest >= count - 1 else 0
    counts, rest = [largest] + [least] * (count - 1), total - largest - least * (count - 1)
    while rest > 0:
        free = [i for i in range(1, count) if counts[i] < largest] or [i for i in range(1, count) if counts[i] < limit]
        mass, budget = sum([weights[i] for i in free]), rest
        for i in free:
            extra = min(limit - counts[i], max(1, budget * weights[i] // mass), rest)
            counts[i] = counts[i] + extra
            rest = rest - extra
    return np.array(counts)


def normal_values(rng, extent, scale, reach, pieces=(), held_as=jnp.bfloat16):
    loudness = levels(rng, extent, pieces, -0.22, 0.18) if pieces else 1.0
    drawn = jax.random.normal(rng, extent, jnp.float32) * scale * loudness
    return jnp.minimum(jnp.maximum(drawn, -reach), reach).astype(held_as)


def setup_inputs(seed: int = 0) -> dict:
    splits = jax.random.split(jax.random.key(seed), 8)
    a_blocks = normal_values(splits[0], (N_ROW, N_COL, BK, NA, BS, BS), 1.0, 6.0, ((0, 8), (1, 16)))
    a_rows = draw_a_rows(jax.random.fold_in(splits[7], 71), 0)
    b_blocks = normal_values(splits[2], (N_ROW, N_COL, 2, BK, NBB, BS, BS), (NB * BS // 2) ** -0.5, 0.09375, ((0, 8), (1, 16)))
    b_cols = draw_b_cols(jax.random.fold_in(splits[7], 71), 0)
    screen = plant((jax.random.randint(splits[4], (N_ROW, N_COL, N_COL, BK, NA, NBB), 0, 4) < 3).astype(jnp.int32), jax.random.fold_in(splits[4], 1), 0, 1)
    keep = plant((jax.random.randint(splits[5], (N_ROW, N_COL, 2 * BK * BK), 0, 4) < 3).astype(jnp.int32), jax.random.fold_in(splits[5], 1), 0, 1)
    owners_keys = jax.random.split(jax.random.fold_in(splits[6], 1), N_ROW * N_COL * (2 * BK * BK) // (2 * BK * BK))
    owners_turns = jax.random.permutation(jax.random.fold_in(splits[6], 3), N_ROW * N_COL * (2 * BK * BK) // (2 * BK * BK))
    owners = jax.vmap(lambda own, number: shared_out(jax.random.fold_in(splits[6], 2), own, number, 2 * BK * BK, N_COL, 1, SLOT, 2))(owners_keys, owners_turns).reshape((N_ROW, N_COL, 2 * BK * BK, 1))
    return dict(a_blocks=a_blocks, a_rows=a_rows, b_blocks=b_blocks, b_cols=b_cols, screen=screen, keep=keep, owners=owners)


def tile_product(a_data, a_list, b_data, b_list, screen_now, rows_count, cols_count):
    prod = jnp.einsum('kaxy,kbyz->kabxz', a_data.astype(jnp.float32), b_data.astype(jnp.float32))
    prod = prod * screen_now.astype(jnp.float32)[:, :, :, None, None]
    row_hot = (a_list[:, :, None] == jnp.arange(rows_count, dtype=jnp.int32)).astype(jnp.float32)
    col_hot = (b_list[:, :, None] == jnp.arange(cols_count, dtype=jnp.int32)).astype(jnp.float32)
    placed = jnp.einsum('kar,kabxz->krbxz', row_hot, prod, precision=lax.Precision.HIGHEST)
    return jnp.einsum('kbc,krbxz->rcxz', col_hot, placed, precision=lax.Precision.HIGHEST)


def route_blocks(tile, keep_row, owner_row, dest_count, slot_count):
    count = owner_row.shape[0]
    order = jnp.arange(count, dtype=jnp.int32)
    same = (owner_row[:, None] == owner_row[None, :]) & (order[None, :] < order[:, None])
    rank = jnp.sum(same.astype(jnp.int32), axis=1).astype(jnp.int32)
    dest_hot = owner_row[:, None] == jnp.arange(dest_count, dtype=jnp.int32)
    slot_hot = rank[:, None] == jnp.arange(slot_count, dtype=jnp.int32)
    table = (dest_hot[:, :, None] & slot_hot[:, None, :]).astype(jnp.float32) * keep_row.astype(jnp.float32)[:, None, None]
    sent = jnp.einsum('mos,mxz->osxz', table, tile.astype(jnp.float32), precision=lax.Precision.HIGHEST)
    return sent.astype(jnp.bfloat16)


def reference(a_blocks, a_rows, b_blocks, b_cols, screen, keep, owners):
    grid_rows = a_blocks.shape[0]
    grid_cols = a_blocks.shape[1]
    inner = a_blocks.shape[2]
    rows_tile = 2 * inner
    width = a_blocks.shape[-1]

    def one_tile(flat):
        i = flat // grid_cols
        j = flat % grid_cols

        def advance(total, s):
            g = (j + s) % grid_cols
            e = (i + s) % grid_cols
            p = e % grid_rows
            h = e // grid_rows
            term = tile_product(a_blocks[i, g], a_rows[i, g], b_blocks[p, j, h], b_cols[p, j, h], screen[i, j, s], rows_tile, inner)
            return total + term, None

        start = jnp.zeros((rows_tile, inner, width, width), jnp.float32)
        total, _ = lax.scan(advance, start, jnp.arange(grid_cols, dtype=jnp.int32))
        tile = total.astype(jnp.bfloat16).reshape(rows_tile * inner, width, width)
        return route_blocks(tile, keep[i, j], owners[i, j, :, 0], grid_cols, SLOT)

    sends = lax.map(one_tile, jnp.arange(grid_rows * grid_cols, dtype=jnp.int32))
    sends = sends.reshape(grid_rows, grid_cols, grid_cols, SLOT, width, width)
    return jnp.swapaxes(sends, 1, 2)
```

```python
import functools

import jax
import jax.numpy as jnp
from jax import lax
from jax.experimental import pallas as pl
from jax.experimental.pallas import tpu as pltpu
from jax.sharding import PartitionSpec as P

MESH = pl.DeviceIdType.MESH
BF16, F32, I32 = jnp.bfloat16, jnp.float32, jnp.int32
W = 128

A_PIECES = ((0, 7), (7, 7), (14, 4), (18, 3), (21, 7))
B_PIECES = ((0, 6), (6, 6), (12, 6), (18, 6))
A_HALF = ((0, 1), (2, 3, 4))
UNIT = 0.624


def a_slot(dy, dz, dk):
    return (dy % 4) * 4 + dz * 2 + dk


def b_slot(dx, dz):
    return (dx % 4) * 2 + dz


def a_forwards(dy, dz, p):
    out = []
    if (dy, dz) == (0, 0):
        out += [("y+", a_slot(3, 0, 0)), ("y-", a_slot(1, 0, 0)), ("zl", a_slot(0, 1, 0))]
    elif (dy, dz) == (0, 1):
        if p >= 1:
            out += [("y+", a_slot(3, 1, 0)), ("y-", a_slot(1, 1, 0))]
    elif dz == 0:
        if dy == 3 and p in (0, 1):
            out.append(("y+", a_slot(2, 0, 0)))
        if dy == 1 and p in (2, 3, 4):
            out.append(("y-", a_slot(2, 0, 0)))
        if p == 0:
            out.append(("zl", a_slot(dy, 1, 0)))
    else:
        if dy == 3 and p in (1, 2):
            out.append(("y+", a_slot(2, 1, 0)))
        if dy == 1 and p in (3, 4):
            out.append(("y-", a_slot(2, 1, 0)))
    out.append(("sib", a_slot(dy, dz, 1)))
    return out


def b_forwards(dx, dz, c):
    if (dx, dz) == (0, 0):
        return [("x+", b_slot(3, 0)), ("x-", b_slot(1, 0)), ("zh", b_slot(0, 1))]
    if dx == 0:
        return [("x+", b_slot(3, 1)), ("x-", b_slot(1, 1))]
    if dx == 3 and c in (0, 1):
        return [("x+", b_slot(2, dz))]
    if dx == 1 and c in (2, 3):
        return [("x-", b_slot(2, dz))]
    return []


def arrivals():
    ends = [lo + n for lo, n in A_PIECES]
    out = []

    def a(dy, dz, p, t):
        out.append((t, "A", a_slot(dy, dz, 0), p))
        out.append((t + 2.0, "A", a_slot(dy, dz, 1), p))

    for p in range(5):
        out.append((1.5 + ends[p] * 0.1, "A", a_slot(0, 0, 1), p))
        a(1, 0, p, UNIT * ends[p])
        a(3, 0, p, UNIT * ends[p])
        a(0, 1, p, 2 * UNIT * ends[p] * 0.92)
        a(2, 0, p, UNIT * (28 + (ends[p] if p < 2 else ends[p] - 14)))
        if p:
            a(1, 1, p, UNIT * (42 + ends[p] - 7))
            a(3, 1, p, UNIT * (42 + ends[p] - 7))
            a(2, 1, p, UNIT * (63 + (ends[p] - 7 if p < 3 else ends[p] - 18)))
    a(1, 1, 0, UNIT * 58)
    a(3, 1, 0, UNIT * 60)
    a(2, 1, 0, UNIT * 70)
    for c in range(4):
        e = 6 * (c + 1)
        half = 6 * (c % 2 + 1)
        for dx in (1, 3):
            out.append((UNIT * e, "B", b_slot(dx, 0), c))
            out.append((UNIT * (36 + e), "B", b_slot(dx, 1), c))
        out.append((2 * UNIT * e, "B", b_slot(0, 1), c))
        out.append((UNIT * (24 + half), "B", b_slot(2, 0), c))
        out.append((UNIT * (60 + half), "B", b_slot(2, 1), c))
    return sorted(out, key=lambda r: r[0])


def make_plan(step):
    phases, copies = [[]], []

    def start(kind, slot, piece, phase):
        if kind == "A":
            dy, dz, dk = slot // 4, slot // 2 % 2, slot % 2
            nexts = [] if dk else a_forwards(dy, dz, piece)
        else:
            nexts = b_forwards(slot // 2, slot % 2, piece)
        for target, there in nexts:
            copies.append((phase, kind, slot, there, piece, target))

    for p in range(5):
        start("A", 0, p, 0)
        if p < 4:
            start("B", 0, p, 0)
    last = 0.0
    for t, kind, slot, piece in arrivals():
        if t - last > step or not phases[-1]:
            if phases[-1]:
                last = t
            phases.append([])
            last = t
        phases[-1].append((kind, slot, piece))
        start(kind, slot, piece, len(phases) - 1)
    when_a = [0] * 32
    when_b = [0] * 32
    for n, phase in enumerate(phases):
        for kind, slot, piece in phase:
            if kind == "A":
                at = slot * 2 + (0 if piece in A_HALF[0] else 1)
                when_a[at] = max(when_a[at], n)
            else:
                at = slot * 4 + piece
                when_b[at] = max(when_b[at], n)
    triggers, bounds = [], [0]
    for n in range(len(phases)):
        triggers += [i for i in range(32) if when_a[i] == n]
        triggers += [32 + i for i in range(32) if when_b[i] == n]
        bounds.append(len(triggers))
    return phases, copies, when_a, when_b, triggers, bounds


PHASES, COPIES, WHEN_A, WHEN_B, TRIGGERS, BOUNDS = make_plan(2.4)


def entry(table, at):
    padded = list(table) + [0] * (-len(table) % 4)
    words = [sum(v << (7 * i) for i, v in enumerate(padded[w:w + 4])) for w in range(0, len(padded), 4)]
    which, word = lax.div(at, 4), I32(words[0])
    for i, v in enumerate(words[1:], 1):
        word = jnp.where(which == i, I32(v), word)
    return lax.rem(lax.shift_right_logical(word, 7 * lax.rem(at, 4)), 128)


def kernel(a_in, b_in, a_rows, b_cols, screen, keep, owners, out, a_all, b_all, total, dense, stage, lists, mask, meta_a,
           meta_b, owned_m, owned_f, a_recv, b_recv, sent, ma_send, ma_recv, mb_send, mb_recv, out_send, out_recv, own_sem):
    row, col = lax.axis_index("row"), lax.axis_index("col")
    rem, div = lax.rem, lax.div
    x, zh = div(row, 2), rem(row, 2)
    y, zl, core = div(col, 4), rem(div(col, 2), 2), rem(col, 2)
    targets = {
        "y+": (row, rem(col + 4, 16)),
        "y-": (row, rem(col + 12, 16)),
        "zl": (row, col + 2 - 4 * zl),
        "sib": (row, col + 1 - 2 * core),
        "x+": (rem(row + 2, 8), col),
        "x-": (rem(row + 6, 8), col),
        "zh": (row + 1 - 2 * zh, col),
    }

    barrier = pltpu.get_barrier_semaphore()

    @pl.loop(1, 16)
    def _(t):
        pl.semaphore_signal(barrier, inc=1, device_id=(row, rem(col + t, 16)), device_id_type=MESH)

    @pl.loop(1, 8)
    def _(t):
        pl.semaphore_signal(barrier, inc=1, device_id=(rem(row + t, 8), col), device_id_type=MESH)

    for i in list(range(36, 64)) + list(range(104, W)):
        lists[i] = I32(0)
    for k in range(4):
        gone = I32(28)
        places = [I32(7)] * 8
        for a in range(7):
            at = a_rows[k, a]
            gone = gone - at
            places = [jnp.where(at == r, a, v) for r, v in enumerate(places)]
        for r in range(8):
            lists[k * 8 + r] = places[r]
        lists[32 + k] = gone
    for h in range(2):
        for k in range(4):
            gone = I32(6)
            places = [I32(3)] * 4
            for b in range(3):
                at = b_cols[b, h, k]
                gone = gone - at
                places = [jnp.where(at == c, b, v) for c, v in enumerate(places)]
            for c in range(4):
                lists[64 + h * 16 + k * 4 + c] = places[c]
            lists[96 + h * 4 + k] = gone

    @pl.loop(0, W)
    def _(i):
        meta_a[col, i] = lists[i]
        meta_b[row, i] = lists[i]

    @pl.loop(0, 28)
    def _(i):
        k, n = div(i, 7), rem(i, 7)
        place = n + jnp.where(n >= lists[32 + k], 1, 0)
        a_all[0, i] = a_in[k, jnp.minimum(lists[k * 8 + place], 6)]

    @pl.loop(0, 24)
    def _(i):
        hk, n = div(i, 3), rem(i, 3)
        place = n + jnp.where(n >= lists[96 + hk], 1, 0)
        b_all[0, i] = b_in[hk, jnp.minimum(lists[64 + hk * 4 + place], 2)]

    def copy_of(number):
        _, kind, slot, there, piece, target = COPIES[number]
        ref, pieces, recv = (a_all, A_PIECES, a_recv) if kind == "A" else (b_all, B_PIECES, b_recv)
        lo, n = pieces[piece]
        return pltpu.make_async_remote_copy(
            src_ref=ref.at[slot, pl.ds(lo, n)], dst_ref=ref.at[there, pl.ds(lo, n)],
            send_sem=sent.at[number], recv_sem=recv.at[there * len(pieces) + piece],
            device_id=targets[target], device_id_type=MESH)

    def arrival_of(kind, slot, piece):
        ref, pieces, recv = (a_all, A_PIECES, a_recv) if kind == "A" else (b_all, B_PIECES, b_recv)
        lo, n = pieces[piece]
        there = ref.at[slot, pl.ds(lo, n)]
        return pltpu.make_async_remote_copy(
            src_ref=there, dst_ref=there, send_sem=sent.at[0], recv_sem=recv.at[slot * len(pieces) + piece],
            device_id=targets["sib"], device_id_type=MESH)

    def meta_a_copy(t):
        return pltpu.make_async_remote_copy(
            src_ref=lists, dst_ref=meta_a.at[col], send_sem=ma_send.at[t], recv_sem=ma_recv.at[col],
            device_id=(row, rem(col + t, 16)), device_id_type=MESH)

    def meta_b_copy(t):
        return pltpu.make_async_remote_copy(
            src_ref=lists, dst_ref=meta_b.at[row], send_sem=mb_send.at[t], recv_sem=mb_recv.at[row],
            device_id=(rem(row + t, 8), col), device_id_type=MESH)

    pl.semaphore_wait(barrier, 22)

    for number, copy in enumerate(COPIES):
        if copy[0] == 0:
            copy_of(number).start()

    @pl.loop(1, 16)
    def _(t):
        meta_a_copy(t).start()

    @pl.loop(1, 8)
    def _(t):
        meta_b_copy(t).start()

    @pl.loop(0, 16)
    def _(s):
        for k in range(4):
            for a in range(8):
                for b in range(4):
                    at = (s * 4 + k) * 32 + a * 4 + b
                    mask[at] = screen[a, b, k, s].astype(F32) if a < 7 and b < 3 else F32(0)

    @pl.loop(0, 16)
    def _(o):
        first, last = I32(32), I32(-1)
        for m in range(32):
            here = owners[m] == o
            first = jnp.where(here, jnp.minimum(first, m), first)
            last = jnp.where(here, m, last)
        some, two = last >= 0, last > first
        first = jnp.where(some, first, 0)
        last = jnp.where(two, last, 0)
        owned_m[2 * o] = rem(first, 4) * 8 + div(first, 4)
        owned_m[2 * o + 1] = rem(last, 4) * 8 + div(last, 4)
        owned_f[2 * o] = jnp.where(some, keep[first], 0).astype(F32)
        owned_f[2 * o + 1] = jnp.where(two, keep[last], 0).astype(F32)

    @pl.loop(0, 32)
    def _(m):
        total[m] = jnp.zeros((W, W), F32)

    @pl.loop(1, 16)
    def _(t):
        source = rem(col + t, 16)
        pltpu.make_async_remote_copy(
            src_ref=meta_a.at[source], dst_ref=meta_a.at[source], send_sem=ma_send.at[t], recv_sem=ma_recv.at[source],
            device_id=(row, source), device_id_type=MESH).wait_recv()

    @pl.loop(1, 8)
    def _(t):
        source = rem(row + t, 8)
        pltpu.make_async_remote_copy(
            src_ref=meta_b.at[source], dst_ref=meta_b.at[source], send_sem=mb_send.at[t], recv_sem=mb_recv.at[source],
            device_id=(source, col), device_id_type=MESH).wait_recv()

    def multiply(qa, half, qb, h, s, g, p):
        for kk in range(2):
            k = half * 2 + kk
            gone = meta_a[g, 32 + k]
            for r in range(8):
                low = a_all[qa, k * 7 + min(r, 6)]
                high = a_all[qa, k * 7 + max(r - 1, 0)]
                dense[r * W:(r + 1) * W, kk * W:(kk + 1) * W] = jnp.where(r < gone, low, high)
        for c in range(4):
            right = []
            for kk in range(2):
                hk = h * 4 + half * 2 + kk
                low = b_all[qb, hk * 3 + min(c, 2)]
                high = b_all[qb, hk * 3 + max(c - 1, 0)]
                right.append(jnp.where(c < meta_b[p, 96 + hk], low, high))
            rows = []
            for r in range(8):
                cells = []
                for kk in range(2):
                    k = half * 2 + kk
                    at = (s * 4 + k) * 32 + meta_a[g, k * 8 + r] * 4 + meta_b[p, 64 + h * 16 + k * 4 + c]
                    cells.append(dense[r * W:(r + 1) * W, kk * W:(kk + 1) * W] * mask[at].astype(BF16))
                rows.append(jnp.concatenate(cells, axis=1))
            left = jnp.concatenate(rows, axis=0)
            part = jnp.dot(left, jnp.concatenate(right, axis=0), preferred_element_type=F32)
            total[c * 8:(c + 1) * 8] += part.reshape(8, W, W)

    @pl.loop(0, len(PHASES))
    def _(n):
        for i, phase in enumerate(PHASES):
            if i == 0:
                continue

            @pl.when(n == i)
            def _(i=i, phase=phase):
                for kind, slot, piece in phase:
                    arrival_of(kind, slot, piece).wait_recv()
                    for number, copy in enumerate(COPIES):
                        if copy[0] == i and (copy[1], copy[2], copy[4]) == (kind, slot, piece):
                            copy_of(number).start()

        @pl.loop(entry(BOUNDS, n), entry(BOUNDS, n + 1))
        def _(u):
            code = entry(TRIGGERS, u)
            by_b = div(code, 32)
            index = rem(code, 32)
            half = rem(index, 2)
            which = div(index, 2)
            g_a = 4 * rem(y + div(which, 4), 4) + 2 * rem(zl + rem(div(which, 2), 2), 2) + rem(core + rem(which, 2), 2)
            s_a = rem(g_a - col + 16, 16)
            p_b = 2 * rem(x + div(which, 4), 4) + rem(zh + rem(div(which, 2), 2), 2)
            s_b = rem(p_b + 8 * rem(which, 2) - row + 16, 16)
            s = jnp.where(by_b == 1, s_b, s_a)
            g = rem(col + s, 16)
            e = rem(row + s, 16)
            p, h = rem(e, 8), div(e, 8)
            qa = 4 * rem(div(g, 4) - y + 4, 4) + 2 * rem(rem(div(g, 2), 2) + zl, 2) + rem(rem(g, 2) + core, 2)
            qb = 2 * rem(div(p, 2) - x + 4, 4) + rem(rem(p, 2) + zh, 2)
            when_a = entry(WHEN_A, qa * 2 + half)
            when_b = entry(WHEN_B, qb * 4 + h * 2 + half)
            ready = jnp.where(by_b == 1, when_a < n, when_b <= n)

            @pl.when(ready)
            def _():
                multiply(qa, half, qb, h, s, g, p)

    def out_copy(t):
        o = rem(col + t, 16)
        return pltpu.make_async_remote_copy(
            src_ref=stage.at[t], dst_ref=out.at[col], send_sem=out_send.at[t], recv_sem=out_recv.at[col],
            device_id=(row, o), device_id_type=MESH)

    @pl.loop(0, 16)
    def _(u):
        t = rem(u + 8, 16)
        o = rem(col + t, 16)
        for slot in range(2):
            stage[t, slot] = (total[owned_m[2 * o + slot]] * owned_f[2 * o + slot]).astype(BF16)

        @pl.when(t != 0)
        def _():
            out_copy(t).start()

        @pl.when(t == 0)
        def _():
            pltpu.make_async_copy(stage.at[0], out.at[col], own_sem).start()

    pltpu.make_async_copy(stage.at[0], out.at[col], own_sem).wait()

    @pl.loop(1, 16)
    def _(t):
        meta_a_copy(t).wait_send()
        out_copy(t).wait_send()

    @pl.loop(1, 8)
    def _(t):
        meta_b_copy(t).wait_send()

    for number in range(len(COPIES)):
        copy_of(number).wait_send()

    @pl.loop(1, 16)
    def _(t):
        source = rem(col + t, 16)
        pltpu.make_async_remote_copy(
            src_ref=stage.at[t], dst_ref=out.at[source], send_sem=out_send.at[t], recv_sem=out_recv.at[source],
            device_id=(row, source), device_id_type=MESH).wait_recv()


def on_device(a_blocks, a_rows, b_blocks, b_cols, screen, keep, owners):
    vmem, smem = pl.BlockSpec(memory_space=pltpu.VMEM), pl.BlockSpec(memory_space=pltpu.SMEM)
    dma = pltpu.SemaphoreType.DMA
    out = pl.pallas_call(
        kernel,
        out_shape=jax.ShapeDtypeStruct((16, 2, W, W), BF16),
        in_specs=[vmem, vmem, smem, smem, smem, smem, smem],
        out_specs=pl.BlockSpec(memory_space=pl.ANY),
        scratch_shapes=[
            pltpu.VMEM((16, 28, W, W), BF16),
            pltpu.VMEM((8, 24, W, W), BF16),
            pltpu.VMEM((32, W, W), F32),
            pltpu.VMEM((8 * W, 2 * W), BF16),
            pltpu.VMEM((16, 2, W, W), BF16),
            pltpu.SMEM((W,), I32),
            pltpu.SMEM((2048,), F32),
            pltpu.SMEM((16, W), I32),
            pltpu.SMEM((8, W), I32),
            pltpu.SMEM((32,), I32),
            pltpu.SMEM((32,), F32),
            dma((16 * len(A_PIECES),)),
            dma((8 * len(B_PIECES),)),
            dma((len(COPIES),)),
            dma((16,)),
            dma((16,)),
            dma((8,)),
            dma((8,)),
            dma((16,)),
            dma((16,)),
            dma,
        ],
        compiler_params=pltpu.CompilerParams(
            collective_id=0, has_side_effects=True, vmem_limit_bytes=48 * 2**20),
        cost_estimate=pl.CostEstimate(flops=8_600_000_000, bytes_accessed=4_000_000, transcendentals=0),
        name="gather_multiply_send",
    )(
        a_blocks[0, 0], b_blocks[0, 0].reshape(8, 3, W, W), a_rows[0, 0], jnp.transpose(b_cols[0, 0], (2, 0, 1)),
        jnp.transpose(screen[0, 0], (2, 3, 1, 0)), keep[0, 0], owners[0, 0, :, 0],
    )
    return out[None, None]


def solution(mesh):
    in_specs = (
        P("row", "col", None, None, None, None),
        P("row", "col", None, None),
        P("row", "col", None, None, None, None, None),
        P("row", "col", None, None, None),
        P("row", "col", None, None, None, None),
        P("row", "col", None),
        P("row", "col", None, None),
    )
    out_specs = P("row", "col", None, None, None, None)
    return jax.shard_map(
        on_device, mesh=mesh, in_specs=in_specs, out_specs=out_specs, check_vma=False
    )
```

```python
import functools

import jax
import jax.numpy as jnp
from jax import lax
from jax.experimental import pallas as pl
from jax.experimental.pallas import tpu as pltpu
from jax.sharding import PartitionSpec as P

MESH = pl.DeviceIdType.MESH
BF16, F32, I32 = jnp.bfloat16, jnp.float32, jnp.int32
W = 128

A_PIECES = ((0, 7), (7, 7), (14, 4), (18, 3), (21, 7))
B_PIECES = ((0, 6), (6, 6), (12, 6), (18, 6))
A_HALF = ((0, 1), (2, 3, 4))


def a_slot(dy, dz, dk):
    return (dy % 4) * 4 + dz * 2 + dk


def b_slot(dx, dz):
    return (dx % 4) * 2 + dz


def a_forwards(dy, dz, p):
    out = []
    if (dy, dz) == (0, 0):
        out += [("y+", a_slot(3, 0, 0)), ("y-", a_slot(1, 0, 0)), ("zl", a_slot(0, 1, 0))]
    elif (dy, dz) == (0, 1):
        if p >= 1:
            out += [("y+", a_slot(3, 1, 0)), ("y-", a_slot(1, 1, 0))]
    elif dz == 0:
        if dy == 3 and p in (0, 1):
            out.append(("y+", a_slot(2, 0, 0)))
        if dy == 1 and p in (2, 3, 4):
            out.append(("y-", a_slot(2, 0, 0)))
        if p == 0:
            out.append(("zl", a_slot(dy, 1, 0)))
    else:
        if dy == 3 and p in (1, 2):
            out.append(("y+", a_slot(2, 1, 0)))
        if dy == 1 and p in (3, 4):
            out.append(("y-", a_slot(2, 1, 0)))
    out.append(("sib", a_slot(dy, dz, 1)))
    return out


def b_forwards(dx, dz, c):
    if (dx, dz) == (0, 0):
        return [("x+", b_slot(3, 0)), ("x-", b_slot(1, 0)), ("zh", b_slot(0, 1))]
    if dx == 0:
        return [("x+", b_slot(3, 1)), ("x-", b_slot(1, 1))]
    if dx == 3 and c in (0, 1):
        return [("x+", b_slot(2, dz))]
    if dx == 1 and c in (2, 3):
        return [("x-", b_slot(2, dz))]
    return []


ORDER = (
    ((0, 1, 0), (0, 1, 1), (0, 1, 2), (1, 2, 0), (1, 6, 0), (0, 1, 3),),
    ((0, 1, 4), (0, 4, 0), (0, 12, 0),),
    ((1, 1, 0), (1, 2, 1), (1, 6, 1), (0, 13, 0),),
    ((0, 2, 0), (0, 5, 0), (0, 4, 1), (0, 12, 1),),
    ((0, 4, 2), (0, 12, 2), (1, 2, 2), (1, 6, 2),),
    ((0, 3, 0), (0, 13, 1), (0, 4, 3), (0, 12, 3), (0, 5, 1),),
    ((1, 1, 1), (0, 13, 2), (1, 2, 3), (1, 6, 3), (0, 5, 2),),
    ((0, 13, 3), (0, 5, 3), (0, 2, 1), (0, 4, 4), (0, 12, 4),),
    ((1, 3, 0), (1, 4, 0),),
    ((0, 8, 2),),
    ((0, 3, 1), (0, 13, 4), (0, 8, 0), (0, 8, 3), (0, 5, 4), (1, 1, 2),),
    ((0, 2, 2), (1, 4, 2), (1, 7, 0),),
    ((0, 9, 2),),
    ((0, 9, 0), (0, 9, 3), (0, 2, 3), (0, 3, 2), (0, 6, 1), (0, 8, 1), (1, 3, 1), (1, 4, 1),),
    ((1, 1, 3), (0, 3, 3), (1, 4, 3), (1, 7, 1), (0, 9, 1), (0, 8, 4), (0, 14, 1), (0, 7, 1),),
    ((0, 2, 4), (0, 6, 2), (0, 14, 2),),
    ((1, 3, 2), (1, 7, 2), (0, 15, 1),),
    ((0, 6, 3), (0, 14, 3), (0, 9, 4),),
    ((0, 3, 4), (0, 14, 0), (0, 15, 2), (0, 7, 2),),
    ((1, 3, 3), (1, 5, 0),),
    ((0, 15, 3), (0, 7, 3), (0, 6, 4), (0, 10, 1),),
    ((0, 15, 0), (0, 6, 0), (0, 10, 3), (1, 5, 2), (1, 7, 3),),
    ((0, 11, 1), (0, 14, 4), (0, 7, 4),),
    ((1, 5, 1), (1, 5, 3), (0, 7, 0), (0, 11, 3), (0, 10, 0), (0, 10, 4),),
    ((0, 10, 2),),
    ((0, 15, 4),),
    ((0, 11, 0), (0, 11, 4), (0, 11, 2),),
)


def make_plan():
    phases, copies = [[]] + [[("AB"[kind], slot, piece) for kind, slot, piece in phase] for phase in ORDER], []

    def start(kind, slot, piece, phase):
        if kind == "A":
            dy, dz, dk = slot // 4, slot // 2 % 2, slot % 2
            nexts = [] if dk else a_forwards(dy, dz, piece)
        else:
            nexts = b_forwards(slot // 2, slot % 2, piece)
        for target, there in nexts:
            copies.append((phase, kind, slot, there, piece, target))

    for p in range(5):
        start("A", 0, p, 0)
        if p < 4:
            start("B", 0, p, 0)
    for n, phase in enumerate(phases):
        for kind, slot, piece in phase:
            start(kind, slot, piece, n)
    when_a = [0] * 32
    when_b = [0] * 32
    for n, phase in enumerate(phases):
        for kind, slot, piece in phase:
            if kind == "A":
                at = slot * 2 + (0 if piece in A_HALF[0] else 1)
                when_a[at] = max(when_a[at], n)
            else:
                at = slot * 4 + piece
                when_b[at] = max(when_b[at], n)
    triggers, bounds = [], [0]
    for n in range(len(phases)):
        triggers += [i for i in range(32) if when_a[i] == n]
        triggers += [32 + i for i in range(32) if when_b[i] == n]
        bounds.append(len(triggers))
    return phases, copies, when_a, when_b, triggers, bounds


PHASES, COPIES, WHEN_A, WHEN_B, TRIGGERS, BOUNDS = make_plan()


def entry(table, at):
    padded = list(table) + [0] * (-len(table) % 4)
    words = [sum(v << (7 * i) for i, v in enumerate(padded[w:w + 4])) for w in range(0, len(padded), 4)]
    which, word = lax.div(at, 4), I32(words[0])
    for i, v in enumerate(words[1:], 1):
        word = jnp.where(which == i, I32(v), word)
    return lax.rem(lax.shift_right_logical(word, 7 * lax.rem(at, 4)), 128)


def kernel(a_hbm, b_hbm, a_rows, b_cols, screen, keep, owners, out, a_in, b_in, a_all, b_all, total, dense, stage, lists, meta_a,
           meta_b, owned_m, owned_f, a_recv, b_recv, sent, ma_send, ma_recv, mb_send, mb_recv, out_send, out_recv, own_sem, in_sem):
    row, col = lax.axis_index("row"), lax.axis_index("col")
    rem, div = lax.rem, lax.div
    x, zh = div(row, 2), rem(row, 2)
    y, zl, core = div(col, 4), rem(div(col, 2), 2), rem(col, 2)
    targets = {
        "y+": (row, rem(col + 4, 16)),
        "y-": (row, rem(col + 12, 16)),
        "zl": (row, col + 2 - 4 * zl),
        "sib": (row, col + 1 - 2 * core),
        "x+": (rem(row + 2, 8), col),
        "x-": (rem(row + 6, 8), col),
        "zh": (row + 1 - 2 * zh, col),
    }

    load_a = pltpu.make_async_copy(a_hbm, a_in, in_sem.at[0])
    load_b = pltpu.make_async_copy(b_hbm, b_in, in_sem.at[1])
    load_a.start()
    load_b.start()

    barrier = pltpu.get_barrier_semaphore()

    @pl.loop(1, 16)
    def _(t):
        pl.semaphore_signal(barrier, inc=1, device_id=(row, rem(col + t, 16)), device_id_type=MESH)

    @pl.loop(1, 8)
    def _(t):
        pl.semaphore_signal(barrier, inc=1, device_id=(rem(row + t, 8), col), device_id_type=MESH)

    def note(at, value):
        lists[at] = value
        meta_a[col, at] = value
        meta_b[row, at] = value

    for i in list(range(36, 64)) + list(range(104, W)):
        lists[i] = I32(0)
    for k in range(4):
        gone = I32(28)
        places = [I32(0)] * 8
        for a in range(7):
            at = a_rows[k, a]
            gone = gone - at
            places = [jnp.where(at == r, a, v) for r, v in enumerate(places)]
        for r in range(8):
            note(k * 8 + r, places[r])
        note(32 + k, gone)
    for h in range(2):
        for k in range(4):
            gone = I32(6)
            places = [I32(0)] * 4
            for b in range(3):
                at = b_cols[b, h, k]
                gone = gone - at
                places = [jnp.where(at == c, b, v) for c, v in enumerate(places)]
            for c in range(4):
                note(64 + h * 16 + k * 4 + c, places[c])
            note(96 + h * 4 + k, gone)

    load_a.wait()
    for k in range(4):
        gone = lists[32 + k]
        for n in range(7):
            a_all[0, k * 7 + n] = a_in[k, lists[k * 8 + n + jnp.where(n >= gone, 1, 0)]]
    load_b.wait()
    for hk in range(8):
        gone = lists[96 + hk]
        for n in range(3):
            b_all[0, hk * 3 + n] = b_in[hk, lists[64 + hk * 4 + n + jnp.where(n >= gone, 1, 0)]]

    def copy_of(number):
        _, kind, slot, there, piece, target = COPIES[number]
        ref, pieces, recv = (a_all, A_PIECES, a_recv) if kind == "A" else (b_all, B_PIECES, b_recv)
        lo, n = pieces[piece]
        return pltpu.make_async_remote_copy(
            src_ref=ref.at[slot, pl.ds(lo, n)], dst_ref=ref.at[there, pl.ds(lo, n)],
            send_sem=sent.at[number], recv_sem=recv.at[there * len(pieces) + piece],
            device_id=targets[target], device_id_type=MESH)

    def arrival_of(kind, slot, piece):
        ref, pieces, recv = (a_all, A_PIECES, a_recv) if kind == "A" else (b_all, B_PIECES, b_recv)
        lo, n = pieces[piece]
        there = ref.at[slot, pl.ds(lo, n)]
        return pltpu.make_async_remote_copy(
            src_ref=there, dst_ref=there, send_sem=sent.at[0], recv_sem=recv.at[slot * len(pieces) + piece],
            device_id=targets["sib"], device_id_type=MESH)

    def meta_a_copy(t):
        return pltpu.make_async_remote_copy(
            src_ref=lists, dst_ref=meta_a.at[col], send_sem=ma_send.at[t], recv_sem=ma_recv.at[col],
            device_id=(row, rem(col + t, 16)), device_id_type=MESH)

    def meta_b_copy(t):
        return pltpu.make_async_remote_copy(
            src_ref=lists, dst_ref=meta_b.at[row], send_sem=mb_send.at[t], recv_sem=mb_recv.at[row],
            device_id=(rem(row + t, 8), col), device_id_type=MESH)

    pl.semaphore_wait(barrier, 22)

    @pl.loop(1, 16)
    def _(t):
        meta_a_copy(t).start()

    @pl.loop(1, 8)
    def _(t):
        meta_b_copy(t).start()

    for number, copy in enumerate(COPIES):
        if copy[0] == 0:
            copy_of(number).start()

    @pl.loop(0, 16)
    def _(o):
        first, last = I32(32), I32(-1)
        for m in range(32):
            here = owners[m] == o
            first = jnp.where(here, jnp.minimum(first, m), first)
            last = jnp.where(here, m, last)
        some, two = last >= 0, last > first
        first = jnp.where(some, first, 0)
        last = jnp.where(two, last, 0)
        owned_m[2 * o] = rem(first, 4) * 8 + div(first, 4)
        owned_m[2 * o + 1] = rem(last, 4) * 8 + div(last, 4)
        owned_f[2 * o] = jnp.where(some, keep[first], 0).astype(F32)
        owned_f[2 * o + 1] = jnp.where(two, keep[last], 0).astype(F32)

    @pl.loop(0, 32)
    def _(m):
        total[m] = jnp.zeros((W, W), F32)

    @pl.loop(1, 16)
    def _(t):
        source = rem(col + t, 16)
        pltpu.make_async_remote_copy(
            src_ref=meta_a.at[source], dst_ref=meta_a.at[source], send_sem=ma_send.at[t], recv_sem=ma_recv.at[source],
            device_id=(row, source), device_id_type=MESH).wait_recv()

    @pl.loop(1, 8)
    def _(t):
        source = rem(row + t, 8)
        pltpu.make_async_remote_copy(
            src_ref=meta_b.at[source], dst_ref=meta_b.at[source], send_sem=mb_send.at[t], recv_sem=mb_recv.at[source],
            device_id=(source, col), device_id_type=MESH).wait_recv()

    def multiply(qa, half, qb, h, s, g, p):
        for kk in range(2):
            k = half * 2 + kk
            gone = meta_a[g, 32 + k]
            for r in range(8):
                low = a_all[qa, k * 7 + min(r, 6)]
                high = a_all[qa, k * 7 + max(r - 1, 0)]
                dense[r * W:(r + 1) * W, kk * W:(kk + 1) * W] = jnp.where(
                    r == gone, jnp.zeros_like(low), jnp.where(r < gone, low, high))
        for c in range(4):
            right = []
            for kk in range(2):
                hk = h * 4 + half * 2 + kk
                low = b_all[qb, hk * 3 + min(c, 2)]
                high = b_all[qb, hk * 3 + max(c - 1, 0)]
                gone = meta_b[p, 96 + hk]
                right.append(jnp.where(c == gone, jnp.zeros_like(low), jnp.where(c < gone, low, high)))
            rows = []
            for r in range(8):
                cells = []
                for kk in range(2):
                    k = half * 2 + kk
                    passed = screen[meta_a[g, k * 8 + r], meta_b[p, 64 + h * 16 + k * 4 + c], k, s].astype(F32)
                    cells.append(dense[r * W:(r + 1) * W, kk * W:(kk + 1) * W] * passed.astype(BF16))
                rows.append(jnp.concatenate(cells, axis=1))
            left = jnp.concatenate(rows, axis=0)
            part = jnp.dot(left, jnp.concatenate(right, axis=0), preferred_element_type=F32)
            total[c * 8:(c + 1) * 8] += part.reshape(8, W, W)

    @pl.loop(0, len(PHASES))
    def _(n):
        for i, phase in enumerate(PHASES):
            if i == 0:
                continue

            @pl.when(n == i)
            def _(i=i, phase=phase):
                for kind, slot, piece in phase:
                    arrival_of(kind, slot, piece).wait_recv()
                    for number, copy in enumerate(COPIES):
                        if copy[0] == i and (copy[1], copy[2], copy[4]) == (kind, slot, piece):
                            copy_of(number).start()

        @pl.loop(entry(BOUNDS, n), entry(BOUNDS, n + 1))
        def _(u):
            code = entry(TRIGGERS, u)
            by_b = div(code, 32)
            index = rem(code, 32)
            half = rem(index, 2)
            which = div(index, 2)
            g_a = 4 * rem(y + div(which, 4), 4) + 2 * rem(zl + rem(div(which, 2), 2), 2) + rem(core + rem(which, 2), 2)
            s_a = rem(g_a - col + 16, 16)
            p_b = 2 * rem(x + div(which, 4), 4) + rem(zh + rem(div(which, 2), 2), 2)
            s_b = rem(p_b + 8 * rem(which, 2) - row + 16, 16)
            s = jnp.where(by_b == 1, s_b, s_a)
            g = rem(col + s, 16)
            e = rem(row + s, 16)
            p, h = rem(e, 8), div(e, 8)
            qa = 4 * rem(div(g, 4) - y + 4, 4) + 2 * rem(rem(div(g, 2), 2) + zl, 2) + rem(rem(g, 2) + core, 2)
            qb = 2 * rem(div(p, 2) - x + 4, 4) + rem(rem(p, 2) + zh, 2)
            when_a = entry(WHEN_A, qa * 2 + half)
            when_b = entry(WHEN_B, qb * 4 + h * 2 + half)
            ready = jnp.where(by_b == 1, when_a < n, when_b <= n)

            @pl.when(ready)
            def _():
                multiply(qa, half, qb, h, s, g, p)

    def out_copy(t):
        o = rem(col + t, 16)
        return pltpu.make_async_remote_copy(
            src_ref=stage.at[t], dst_ref=out.at[col], send_sem=out_send.at[t], recv_sem=out_recv.at[col],
            device_id=(row, o), device_id_type=MESH)

    @pl.loop(0, 16)
    def _(u):
        t = rem(u + 8, 16)
        o = rem(col + t, 16)
        for slot in range(2):
            stage[t, slot] = (total[owned_m[2 * o + slot]] * owned_f[2 * o + slot]).astype(BF16)

        @pl.when(t != 0)
        def _():
            out_copy(t).start()

        @pl.when(t == 0)
        def _():
            pltpu.make_async_copy(stage.at[0], out.at[col], own_sem).start()

    pltpu.make_async_copy(stage.at[0], out.at[col], own_sem).wait()

    @pl.loop(1, 16)
    def _(t):
        meta_a_copy(t).wait_send()
        out_copy(t).wait_send()

    @pl.loop(1, 8)
    def _(t):
        meta_b_copy(t).wait_send()

    for number in range(len(COPIES)):
        copy_of(number).wait_send()

    @pl.loop(1, 16)
    def _(t):
        source = rem(col + t, 16)
        pltpu.make_async_remote_copy(
            src_ref=stage.at[t], dst_ref=out.at[source], send_sem=out_send.at[t], recv_sem=out_recv.at[source],
            device_id=(row, source), device_id_type=MESH).wait_recv()


def on_device(a_blocks, a_rows, b_blocks, b_cols, screen, keep, owners):
    hbm, smem = pl.BlockSpec(memory_space=pl.ANY), pl.BlockSpec(memory_space=pltpu.SMEM)
    dma = pltpu.SemaphoreType.DMA
    out = pl.pallas_call(
        kernel,
        out_shape=jax.ShapeDtypeStruct((16, 2, W, W), BF16),
        in_specs=[hbm, hbm, smem, smem, smem, smem, smem],
        out_specs=hbm,
        scratch_shapes=[
            pltpu.VMEM((4, 7, W, W), BF16),
            pltpu.VMEM((8, 3, W, W), BF16),
            pltpu.VMEM((16, 28, W, W), BF16),
            pltpu.VMEM((8, 24, W, W), BF16),
            pltpu.VMEM((32, W, W), F32),
            pltpu.VMEM((8 * W, 2 * W), BF16),
            pltpu.VMEM((16, 2, W, W), BF16),
            pltpu.SMEM((W,), I32),
            pltpu.SMEM((16, W), I32),
            pltpu.SMEM((8, W), I32),
            pltpu.SMEM((32,), I32),
            pltpu.SMEM((32,), F32),
            dma((16 * len(A_PIECES),)),
            dma((8 * len(B_PIECES),)),
            dma((len(COPIES),)),
            dma((16,)),
            dma((16,)),
            dma((8,)),
            dma((8,)),
            dma((16,)),
            dma((16,)),
            dma,
            dma((2,)),
        ],
        compiler_params=pltpu.CompilerParams(
            collective_id=0, has_side_effects=True, vmem_limit_bytes=60 * 2**20),
        cost_estimate=pl.CostEstimate(flops=8_600_000_000, bytes_accessed=4_000_000, transcendentals=0),
        name="gather_multiply_send",
    )(
        a_blocks[0, 0], b_blocks[0, 0].reshape(8, 3, W, W), a_rows[0, 0], jnp.transpose(b_cols[0, 0], (2, 0, 1)),
        jnp.transpose(screen[0, 0], (2, 3, 1, 0)), keep[0, 0], owners[0, 0, :, 0],
    )
    return out[None, None]


def solution(mesh):
    in_specs = (
        P("row", "col", None, None, None, None),
        P("row", "col", None, None),
        P("row", "col", None, None, None, None, None),
        P("row", "col", None, None, None),
        P("row", "col", None, None, None, None),
        P("row", "col", None),
        P("row", "col", None, None),
    )
    out_specs = P("row", "col", None, None, None, None)
    return jax.shard_map(
        on_device, mesh=mesh, in_specs=in_specs, out_specs=out_specs, check_vma=False
    )
```

```python
import functools

import jax
import jax.numpy as jnp
from jax import lax
from jax.experimental import pallas as pl
from jax.experimental.pallas import tpu as pltpu
from jax.sharding import PartitionSpec as P

MESH = pl.DeviceIdType.MESH
BF16, F32, I32 = jnp.bfloat16, jnp.float32, jnp.int32
W = 128

A_PIECES = ((0, 4), (4, 5), (9, 5), (14, 3), (17, 5), (22, 6))
B_PIECES = ((0, 6), (6, 6), (12, 6), (18, 6))
A_HALF = tuple(lo // 14 for lo, _ in A_PIECES)
ORDER = (
    (0, 2, 0), (0, 4, 0), (0, 12, 0), (1, 2, 0), (1, 6, 0), (0, 1, 0), (0, 1, 1), (0, 1, 2), (0, 1, 3), (0, 1, 4),
    (0, 1, 5), (0, 4, 1), (0, 12, 1), (1, 1, 0), (1, 2, 2), (1, 6, 2), (0, 13, 0), (0, 5, 0), (0, 3, 0), (0, 4, 2),
    (0, 12, 2), (0, 2, 1), (0, 4, 3), (0, 13, 1), (0, 8, 0), (1, 4, 0), (0, 5, 1), (1, 3, 0), (0, 12, 3), (1, 1, 2),
    (0, 8, 2), (0, 13, 2), (0, 5, 2), (0, 3, 1), (1, 7, 0), (1, 2, 1), (0, 5, 3), (0, 2, 2), (0, 8, 1), (0, 9, 0),
    (0, 6, 1), (0, 13, 3), (0, 14, 0), (1, 6, 1), (1, 2, 3), (0, 9, 2), (0, 14, 1), (0, 4, 4), (0, 2, 3), (0, 9, 1),
    (0, 8, 3), (0, 3, 2), (0, 7, 1), (0, 12, 4), (1, 6, 3), (1, 4, 2), (0, 6, 0), (0, 15, 0), (0, 15, 1), (0, 6, 2),
    (0, 5, 4), (0, 14, 2), (0, 3, 3), (1, 7, 2), (1, 3, 2), (1, 1, 1), (0, 9, 3), (0, 13, 4), (0, 7, 0), (0, 4, 5),
    (0, 12, 5), (1, 5, 0), (1, 4, 3), (0, 7, 2), (1, 1, 3), (0, 15, 2), (0, 10, 2), (0, 10, 1), (0, 2, 4), (1, 4, 1),
    (1, 5, 2), (0, 5, 5), (0, 13, 5), (0, 8, 4), (0, 8, 5), (0, 2, 5), (1, 7, 1), (0, 11, 2), (1, 3, 1), (0, 11, 1),
    (0, 6, 4), (0, 14, 4), (0, 6, 3), (0, 3, 4), (1, 7, 3), (0, 9, 4), (0, 9, 5), (1, 3, 3), (0, 10, 0), (0, 6, 5),
    (0, 14, 5), (0, 3, 5), (0, 14, 3), (0, 15, 4), (0, 7, 4), (0, 7, 3), (1, 5, 1), (0, 10, 3), (0, 10, 4), (1, 5, 3),
    (0, 11, 0), (0, 10, 5), (0, 15, 5), (0, 7, 5), (0, 15, 3), (0, 11, 3), (0, 11, 4), (0, 11, 5),
)
COPIES = (
    (0, 0, 0, 12, 0, 0), (0, 0, 0, 4, 0, 1), (0, 0, 0, 2, 0, 2), (0, 0, 0, 1, 0, 6), (0, 1, 0, 6, 0, 3), (0, 1, 0, 2, 0, 4),
    (0, 1, 0, 1, 0, 5), (0, 0, 0, 12, 1, 0), (0, 0, 0, 4, 1, 1), (0, 0, 0, 2, 1, 2), (0, 0, 0, 1, 1, 6), (0, 1, 0, 6, 2, 3),
    (0, 1, 0, 2, 2, 4), (0, 1, 0, 1, 2, 5), (0, 0, 0, 12, 2, 0), (0, 0, 0, 4, 2, 1), (0, 0, 0, 2, 2, 2), (0, 0, 0, 1, 2, 6),
    (0, 0, 0, 1, 3, 6), (0, 0, 0, 1, 4, 6), (0, 0, 0, 1, 5, 6), (1, 0, 2, 3, 0, 6), (1, 0, 0, 12, 3, 0), (1, 0, 0, 4, 3, 1),
    (2, 0, 4, 6, 0, 2), (2, 0, 4, 5, 0, 6), (3, 0, 12, 8, 0, 0), (3, 0, 12, 14, 0, 2), (3, 0, 12, 13, 0, 6), (3, 0, 0, 2, 3, 2),
    (5, 1, 6, 4, 0, 3), (5, 1, 0, 1, 1, 5), (5, 1, 0, 1, 3, 5), (12, 0, 4, 5, 1, 6), (13, 0, 12, 8, 1, 0), (13, 0, 12, 13, 1, 6),
    (13, 0, 0, 2, 4, 2), (14, 1, 1, 7, 0, 3), (14, 1, 1, 3, 0, 4), (14, 1, 0, 6, 1, 3), (14, 1, 0, 2, 1, 4), (14, 1, 0, 6, 3, 3),
    (14, 1, 0, 2, 3, 4), (15, 1, 2, 4, 2, 4), (20, 0, 4, 8, 2, 1), (20, 0, 4, 5, 2, 6), (21, 0, 12, 13, 2, 6), (21, 0, 0, 2, 5, 2),
    (22, 0, 2, 14, 1, 0), (22, 0, 2, 6, 1, 1), (22, 0, 2, 3, 1, 6), (22, 0, 0, 12, 4, 0), (22, 0, 0, 4, 4, 1), (23, 0, 4, 8, 3, 1),
    (23, 0, 4, 6, 3, 2), (23, 0, 4, 5, 3, 6), (25, 0, 8, 10, 0, 2), (25, 0, 8, 9, 0, 6), (29, 0, 12, 14, 3, 2), (29, 0, 12, 13, 3, 6),
    (30, 1, 1, 7, 2, 3), (30, 1, 1, 3, 2, 4), (31, 0, 8, 9, 2, 6), (35, 1, 7, 5, 0, 3), (38, 0, 2, 14, 2, 0), (38, 0, 2, 6, 2, 1),
    (38, 0, 2, 3, 2, 6), (38, 0, 0, 12, 5, 0), (38, 0, 0, 4, 5, 1), (39, 0, 8, 9, 1, 6), (41, 0, 6, 7, 1, 6), (43, 0, 14, 15, 0, 6),
    (44, 1, 6, 4, 1, 3), (45, 1, 2, 4, 3, 4), (47, 0, 14, 10, 1, 0), (47, 0, 14, 15, 1, 6), (48, 0, 4, 5, 4, 6), (49, 0, 2, 3, 3, 6),
    (51, 0, 8, 10, 3, 2), (51, 0, 8, 9, 3, 6), (54, 0, 12, 8, 4, 0), (54, 0, 12, 13, 4, 6), (57, 0, 6, 7, 0, 6), (60, 0, 6, 10, 2, 1),
    (60, 0, 6, 7, 2, 6), (62, 0, 14, 15, 2, 6), (65, 1, 3, 5, 2, 4), (66, 1, 1, 7, 1, 3), (66, 1, 1, 3, 1, 4), (70, 0, 4, 8, 5, 1),
    (70, 0, 4, 5, 5, 6), (71, 0, 12, 13, 5, 6), (75, 1, 1, 7, 3, 3), (75, 1, 1, 3, 3, 4), (77, 0, 10, 11, 2, 6), (78, 0, 10, 11, 1, 6),
    (79, 0, 2, 14, 4, 0), (79, 0, 2, 6, 4, 1), (79, 0, 2, 3, 4, 6), (84, 0, 8, 9, 4, 6), (85, 0, 8, 9, 5, 6), (86, 0, 2, 14, 5, 0),
    (86, 0, 2, 6, 5, 1), (86, 0, 2, 3, 5, 6), (87, 1, 7, 5, 1, 3), (91, 0, 6, 7, 4, 6), (92, 0, 14, 10, 4, 0), (92, 0, 14, 15, 4, 6),
    (93, 0, 6, 7, 3, 6), (98, 1, 3, 5, 3, 4), (99, 0, 10, 11, 0, 6), (100, 0, 6, 10, 5, 1), (100, 0, 6, 7, 5, 6), (101, 0, 14, 15, 5, 6),
    (103, 0, 14, 15, 3, 6), (108, 0, 10, 11, 3, 6), (109, 0, 10, 11, 4, 6), (112, 0, 10, 11, 5, 6),
)
TARGETS = ("y+", "y-", "zl", "x+", "x-", "zh", "sib")


def make_plan():
    when_a, when_b, triggers = [0] * 32, [0] * 32, [NOTHING] * (len(ORDER) + 1)
    for n, (kind, slot, piece) in enumerate(ORDER, 1):
        if kind == 0:
            when_a[slot * 2 + A_HALF[piece]] = n
        else:
            when_b[slot * 4 + piece] = n
            triggers[n] = 32 + slot * 4 + piece
    for at in range(2, 32):
        triggers[when_a[at]] = at
    for at in range(2):
        when_a[at] = triggers.index(NOTHING, 1)
        triggers[when_a[at]] = at
    return when_a, when_b, triggers


NOTHING = 127
WHEN_A, WHEN_B, TRIGGERS = make_plan()


def kernel(a_hbm, b_hbm, a_rows, b_cols, screen, keep, owners, out, a_in, b_in, a_all, b_all, total, dense, stage, lists, meta_a,
           meta_b, owned_m, owned_f, a_recv, b_recv, sent, ma_send, ma_recv, mb_send, mb_recv, out_send, out_recv, own_sem, in_sem):
    row, col = lax.axis_index("row"), lax.axis_index("col")
    rem, div = lax.rem, lax.div
    x, zh = div(row, 2), rem(row, 2)
    y, zl, core = div(col, 4), rem(div(col, 2), 2), rem(col, 2)
    targets = {
        "y+": (row, rem(col + 4, 16)),
        "y-": (row, rem(col + 12, 16)),
        "zl": (row, col + 2 - 4 * zl),
        "sib": (row, col + 1 - 2 * core),
        "x+": (rem(row + 2, 8), col),
        "x-": (rem(row + 6, 8), col),
        "zh": (row + 1 - 2 * zh, col),
    }

    load_a = pltpu.make_async_copy(a_hbm, a_in, in_sem.at[0])
    load_b = pltpu.make_async_copy(b_hbm, b_in, in_sem.at[1])
    load_a.start()
    load_b.start()

    barrier = pltpu.get_barrier_semaphore()

    @pl.loop(1, 16)
    def _(t):
        pl.semaphore_signal(barrier, inc=1, device_id=(row, rem(col + t, 16)), device_id_type=MESH)

    @pl.loop(1, 8)
    def _(t):
        pl.semaphore_signal(barrier, inc=1, device_id=(rem(row + t, 8), col), device_id_type=MESH)

    def note(at, value):
        lists[at] = value
        meta_a[col, at] = value
        meta_b[row, at] = value

    for i in list(range(36, 64)) + list(range(104, W)):
        lists[i] = I32(0)
    for k in range(4):
        gone = I32(28)
        places = [I32(0)] * 8
        for a in range(7):
            at = a_rows[k, a]
            gone = gone - at
            places = [jnp.where(at == r, a, v) for r, v in enumerate(places)]
        for r in range(8):
            note(k * 8 + r, places[r])
        note(32 + k, gone)
    for h in range(2):
        for k in range(4):
            gone = I32(6)
            places = [I32(0)] * 4
            for b in range(3):
                at = b_cols[b, h, k]
                gone = gone - at
                places = [jnp.where(at == c, b, v) for c, v in enumerate(places)]
            for c in range(4):
                note(64 + h * 16 + k * 4 + c, places[c])
            note(96 + h * 4 + k, gone)

    load_a.wait()
    for k in range(4):
        gone = lists[32 + k]
        for n in range(7):
            a_all[0, k * 7 + n] = a_in[k, lists[k * 8 + n + jnp.where(n >= gone, 1, 0)]]
    load_b.wait()
    for hk in range(8):
        gone = lists[96 + hk]
        for n in range(3):
            b_all[0, hk * 3 + n] = b_in[hk, lists[64 + hk * 4 + n + jnp.where(n >= gone, 1, 0)]]

    def copy_of(number):
        _, kind, slot, there, piece, target = COPIES[number]
        ref, pieces, recv = (b_all, B_PIECES, b_recv) if kind else (a_all, A_PIECES, a_recv)
        lo, n = pieces[piece]
        return pltpu.make_async_remote_copy(
            src_ref=ref.at[slot, pl.ds(lo, n)], dst_ref=ref.at[there, pl.ds(lo, n)],
            send_sem=sent.at[number], recv_sem=recv.at[there * len(pieces) + piece],
            device_id=targets[TARGETS[target]], device_id_type=MESH)

    def arrival_of(kind, slot, piece):
        ref, pieces, recv = (b_all, B_PIECES, b_recv) if kind else (a_all, A_PIECES, a_recv)
        lo, n = pieces[piece]
        there = ref.at[slot, pl.ds(lo, n)]
        return pltpu.make_async_remote_copy(
            src_ref=there, dst_ref=there, send_sem=sent.at[0], recv_sem=recv.at[slot * len(pieces) + piece],
            device_id=targets["sib"], device_id_type=MESH)

    def meta_a_copy(t):
        return pltpu.make_async_remote_copy(
            src_ref=lists, dst_ref=meta_a.at[col], send_sem=ma_send.at[t], recv_sem=ma_recv.at[col],
            device_id=(row, rem(col + t, 16)), device_id_type=MESH)

    def meta_b_copy(t):
        return pltpu.make_async_remote_copy(
            src_ref=lists, dst_ref=meta_b.at[row], send_sem=mb_send.at[t], recv_sem=mb_recv.at[row],
            device_id=(rem(row + t, 8), col), device_id_type=MESH)

    pl.semaphore_wait(barrier, 22)

    @pl.loop(1, 16)
    def _(t):
        meta_a_copy(t).start()

    @pl.loop(1, 8)
    def _(t):
        meta_b_copy(t).start()

    for number, copy in enumerate(COPIES):
        if copy[0] == 0:
            copy_of(number).start()

    @pl.loop(0, 16)
    def _(o):
        first, last = I32(32), I32(-1)
        for m in range(32):
            here = owners[m] == o
            first = jnp.where(here, jnp.minimum(first, m), first)
            last = jnp.where(here, m, last)
        some, two = last >= 0, last > first
        first = jnp.where(some, first, 0)
        last = jnp.where(two, last, 0)
        owned_m[2 * o] = rem(first, 4) * 8 + div(first, 4)
        owned_m[2 * o + 1] = rem(last, 4) * 8 + div(last, 4)
        owned_f[2 * o] = jnp.where(some, keep[first], 0).astype(F32)
        owned_f[2 * o + 1] = jnp.where(two, keep[last], 0).astype(F32)

    @pl.loop(0, 32)
    def _(m):
        total[m] = jnp.zeros((W, W), F32)

    @pl.loop(1, 16)
    def _(t):
        source = rem(col + t, 16)
        pltpu.make_async_remote_copy(
            src_ref=meta_a.at[source], dst_ref=meta_a.at[source], send_sem=ma_send.at[t], recv_sem=ma_recv.at[source],
            device_id=(row, source), device_id_type=MESH).wait_recv()

    @pl.loop(1, 8)
    def _(t):
        source = rem(row + t, 8)
        pltpu.make_async_remote_copy(
            src_ref=meta_b.at[source], dst_ref=meta_b.at[source], send_sem=mb_send.at[t], recv_sem=mb_recv.at[source],
            device_id=(source, col), device_id_type=MESH).wait_recv()

    def multiply(qa, half, qb, h, s, g, p):
        first = half * 14
        own_rows = [[meta_a[g, half * 16 + kk * 8 + r] for r in range(8)] for kk in range(2)]
        own_cols = [[meta_b[p, 64 + h * 16 + half * 8 + kk * 4 + c] for c in range(4)] for kk in range(2)]
        no_row = [meta_a[g, 32 + half * 2 + kk] for kk in range(2)]
        no_col = [meta_b[p, 96 + h * 4 + half * 2 + kk] for kk in range(2)]
        for kk in range(2):
            for r in range(8):
                low = a_all[qa, first + kk * 7 + min(r, 6)]
                high = a_all[qa, first + kk * 7 + max(r - 1, 0)]
                dense[r * W:(r + 1) * W, kk * W:(kk + 1) * W] = jnp.where(
                    r == no_row[kk], jnp.zeros_like(low), jnp.where(r < no_row[kk], low, high))
        for c in range(4):
            right = []
            for kk in range(2):
                at = h * 12 + half * 6 + kk * 3
                low = b_all[qb, at + min(c, 2)]
                high = b_all[qb, at + max(c - 1, 0)]
                right.append(jnp.where(
                    c == no_col[kk], jnp.zeros_like(low), jnp.where(c < no_col[kk], low, high)))
            rows = []
            for r in range(8):
                cells = []
                for kk in range(2):
                    passed = screen[own_rows[kk][r], own_cols[kk][c], half * 2 + kk, s].astype(F32)
                    cells.append(dense[r * W:(r + 1) * W, kk * W:(kk + 1) * W] * passed.astype(BF16))
                rows.append(jnp.concatenate(cells, axis=1))
            left = jnp.concatenate(rows, axis=0)
            part = jnp.dot(left, jnp.concatenate(right, axis=0), preferred_element_type=F32)
            total[c * 8:(c + 1) * 8] += part.reshape(8, W, W)

    def pair_of(s):
        g, e = rem(col + s, 16), rem(row + s, 16)
        p, h = rem(e, 8), div(e, 8)
        qa = 4 * rem(div(g, 4) - y + 4, 4) + 2 * rem(rem(div(g, 2), 2) + zl, 2) + rem(rem(g, 2) + core, 2)
        qb = 2 * rem(div(p, 2) - x + 4, 4) + rem(rem(p, 2) + zh, 2)
        return g, p, h, qa, qb

    def ready_after(n):
        code = TRIGGERS[n]
        if code == NOTHING:
            return I32(-1)
        half, which = code % 2, code // 2 % 16
        if code < 32:
            g = 4 * rem(y + which // 4, 4) + 2 * rem(zl + which // 2 % 2, 2) + rem(core + which % 2, 2)
            s = rem(g - col + 16, 16)
            _, _, h, _, qb = pair_of(s)
            there = [WHEN_B[at * 2 + half] <= n for at in range(16)]
            at = 2 * qb + h
        else:
            p = 2 * rem(x + which // 4, 4) + rem(zh + which // 2 % 2, 2)
            s = rem(p + 8 * (which % 2) - row + 16, 16)
            at = pair_of(s)[3]
            there = [WHEN_A[at * 2 + half] < n for at in range(16)]
        if not any(there):
            return I32(-1)
        both = rem(lax.shift_right_logical(I32(sum(1 << i for i, v in enumerate(there) if v)), at), 2)
        return jnp.where(both == 1, 2 * s + half, -1)

    def receive(n, low, high):
        if high - low > 1:
            middle = (low + high) // 2
            return lax.cond(n < middle, lambda: receive(n, low, middle), lambda: receive(n, middle, high))
        arrival_of(*ORDER[low - 1]).wait_recv()
        for number, copy in enumerate(COPIES):
            if copy[0] == low:
                copy_of(number).start()
        return ready_after(low)

    @pl.loop(1, len(ORDER) + 1)
    def _(n):
        code = receive(n, 1, len(ORDER) + 1)

        @pl.when(code >= 0)
        def _():
            s, half = div(code, 2), rem(code, 2)
            g, p, h, qa, qb = pair_of(s)
            multiply(qa, half, qb, h, s, g, p)

    def out_copy(t):
        o = rem(col + t, 16)
        return pltpu.make_async_remote_copy(
            src_ref=stage.at[t], dst_ref=out.at[col], send_sem=out_send.at[t], recv_sem=out_recv.at[col],
            device_id=(row, o), device_id_type=MESH)

    @pl.loop(0, 16)
    def _(u):
        t = rem(u + 8, 16)
        o = rem(col + t, 16)
        for slot in range(2):
            stage[t, slot] = (total[owned_m[2 * o + slot]] * owned_f[2 * o + slot]).astype(BF16)

        @pl.when(t != 0)
        def _():
            out_copy(t).start()

        @pl.when(t == 0)
        def _():
            pltpu.make_async_copy(stage.at[0], out.at[col], own_sem).start()

    pltpu.make_async_copy(stage.at[0], out.at[col], own_sem).wait()

    @pl.loop(1, 16)
    def _(t):
        meta_a_copy(t).wait_send()
        out_copy(t).wait_send()

    @pl.loop(1, 8)
    def _(t):
        meta_b_copy(t).wait_send()

    for number in range(len(COPIES)):
        copy_of(number).wait_send()

    @pl.loop(1, 16)
    def _(t):
        source = rem(col + t, 16)
        pltpu.make_async_remote_copy(
            src_ref=stage.at[t], dst_ref=out.at[source], send_sem=out_send.at[t], recv_sem=out_recv.at[source],
            device_id=(row, source), device_id_type=MESH).wait_recv()


def on_device(a_blocks, a_rows, b_blocks, b_cols, screen, keep, owners):
    hbm, smem = pl.BlockSpec(memory_space=pl.ANY), pl.BlockSpec(memory_space=pltpu.SMEM)
    dma = pltpu.SemaphoreType.DMA
    out = pl.pallas_call(
        kernel,
        out_shape=jax.ShapeDtypeStruct((16, 2, W, W), BF16),
        in_specs=[hbm, hbm, smem, smem, smem, smem, smem],
        out_specs=hbm,
        scratch_shapes=[
            pltpu.VMEM((4, 7, W, W), BF16),
            pltpu.VMEM((8, 3, W, W), BF16),
            pltpu.VMEM((16, 28, W, W), BF16),
            pltpu.VMEM((8, 24, W, W), BF16),
            pltpu.VMEM((32, W, W), F32),
            pltpu.VMEM((8 * W, 2 * W), BF16),
            pltpu.VMEM((16, 2, W, W), BF16),
            pltpu.SMEM((W,), I32),
            pltpu.SMEM((16, W), I32),
            pltpu.SMEM((8, W), I32),
            pltpu.SMEM((32,), I32),
            pltpu.SMEM((32,), F32),
            dma((16 * len(A_PIECES),)),
            dma((8 * len(B_PIECES),)),
            dma((len(COPIES),)),
            dma((16,)),
            dma((16,)),
            dma((8,)),
            dma((8,)),
            dma((16,)),
            dma((16,)),
            dma,
            dma((2,)),
        ],
        compiler_params=pltpu.CompilerParams(
            collective_id=0, has_side_effects=True, vmem_limit_bytes=60 * 2**20),
        cost_estimate=pl.CostEstimate(flops=8_600_000_000, bytes_accessed=4_000_000, transcendentals=0),
        name="gather_multiply_send",
    )(
        a_blocks[0, 0], b_blocks[0, 0].reshape(8, 3, W, W), a_rows[0, 0], jnp.transpose(b_cols[0, 0], (2, 0, 1)),
        jnp.transpose(screen[0, 0], (2, 3, 1, 0)), keep[0, 0], owners[0, 0, :, 0],
    )
    return out[None, None]


def solution(mesh):
    in_specs = (
        P("row", "col", None, None, None, None),
        P("row", "col", None, None),
        P("row", "col", None, None, None, None, None),
        P("row", "col", None, None, None),
        P("row", "col", None, None, None, None),
        P("row", "col", None),
        P("row", "col", None, None),
    )
    out_specs = P("row", "col", None, None, None, None)
    return jax.shard_map(
        on_device, mesh=mesh, in_specs=in_specs, out_specs=out_specs, check_vma=False
    )
```

```python
import functools

import jax
import jax.numpy as jnp
from jax import lax
from jax.experimental import pallas as pl
from jax.experimental.pallas import tpu as pltpu
from jax.sharding import PartitionSpec as P

MESH = pl.DeviceIdType.MESH
BF16, F32, I32 = jnp.bfloat16, jnp.float32, jnp.int32
W = 128

A_PIECES = ((0, 4), (4, 5), (9, 5), (14, 3), (17, 5), (22, 6), (0, 14), (14, 14))
B_PIECES = ((0, 6), (6, 6), (12, 6), (18, 6))
A_HALF = tuple(lo // 14 for lo, _ in A_PIECES)
ORDER = (
    (0, 1, 6), (1, 2, 3), (1, 1, 1), (1, 2, 2), (1, 1, 0), (0, 12, 5), (0, 1, 7), (0, 4, 1), (0, 4, 5), (1, 7, 1),
    (0, 12, 2), (0, 4, 3), (0, 12, 1), (1, 3, 1), (1, 6, 1), (0, 12, 3), (1, 4, 2), (0, 12, 4), (0, 4, 2), (0, 12, 0),
    (1, 6, 0), (0, 4, 0), (1, 1, 2), (0, 13, 7), (0, 8, 1), (1, 3, 0), (0, 2, 3), (0, 8, 5), (1, 4, 1), (0, 2, 5),
    (0, 4, 4), (1, 4, 3), (0, 8, 4), (0, 13, 6), (0, 8, 3), (0, 2, 0), (0, 8, 0), (0, 2, 4), (1, 2, 0), (0, 8, 2),
    (0, 2, 1), (0, 2, 2), (1, 7, 0), (0, 9, 7), (0, 5, 7), (1, 5, 1), (1, 3, 2), (0, 9, 6), (0, 3, 7), (0, 3, 6),
    (0, 14, 5), (1, 6, 2), (1, 1, 3), (1, 7, 2), (0, 6, 5), (0, 6, 4), (0, 14, 4), (0, 5, 6), (1, 4, 0), (0, 6, 3),
    (0, 14, 1), (0, 14, 3), (1, 2, 1), (1, 5, 0), (0, 7, 7), (0, 15, 7), (0, 6, 2), (0, 6, 1), (0, 14, 0), (0, 14, 2),
    (1, 5, 2), (0, 6, 0), (1, 7, 3), (1, 3, 3), (0, 15, 6), (0, 10, 5), (0, 10, 3), (0, 10, 4), (0, 7, 6), (1, 6, 3),
    (0, 10, 0), (0, 10, 1), (0, 10, 2), (0, 11, 7), (1, 5, 3), (0, 11, 6),
)
COPIES = (
    (0, 0, 0, 4, 1, 1), (0, 1, 0, 1, 1, 5), (0, 1, 0, 6, 0, 3), (0, 0, 0, 1, 6, 6), (0, 0, 0, 4, 3, 1), (0, 1, 0, 2, 3, 4),
    (0, 0, 0, 12, 5, 0), (0, 1, 0, 6, 1, 3), (0, 0, 0, 4, 5, 1), (1, 0, 0, 4, 4, 1), (1, 0, 0, 4, 2, 1), (1, 0, 0, 12, 1, 0),
    (1, 0, 0, 1, 7, 6), (1, 1, 0, 1, 0, 5), (1, 0, 0, 4, 0, 1), (1, 1, 0, 2, 2, 4), (2, 1, 0, 1, 2, 5), (2, 0, 0, 12, 0, 0),
    (2, 1, 2, 4, 3, 4), (3, 1, 1, 7, 1, 3), (3, 0, 0, 12, 4, 0), (3, 0, 0, 2, 2, 2), (3, 0, 0, 2, 4, 2), (3, 1, 1, 3, 1, 4),
    (4, 1, 2, 4, 2, 4), (5, 1, 1, 7, 0, 3), (5, 1, 1, 3, 0, 4), (8, 0, 0, 12, 2, 0), (8, 0, 0, 2, 3, 2), (9, 0, 0, 2, 5, 2),
    (9, 0, 0, 12, 3, 0), (9, 0, 4, 8, 5, 1), (10, 1, 7, 5, 1, 3), (10, 0, 0, 2, 0, 2), (11, 0, 0, 2, 1, 2), (12, 0, 4, 8, 3, 1),
    (12, 1, 0, 1, 3, 5), (12, 0, 4, 6, 3, 2), (13, 0, 12, 8, 1, 0), (15, 1, 6, 4, 1, 3), (15, 1, 0, 2, 0, 4), (16, 0, 12, 14, 3, 2),
    (18, 0, 12, 8, 4, 0), (18, 0, 12, 13, 7, 6), (19, 0, 4, 8, 2, 1), (20, 0, 12, 14, 0, 2), (20, 0, 12, 8, 0, 0), (20, 0, 12, 13, 6, 6),
    (21, 1, 6, 4, 0, 3), (22, 1, 0, 6, 2, 3), (22, 0, 4, 6, 0, 2), (22, 0, 4, 5, 6, 6), (23, 1, 1, 3, 2, 4), (23, 1, 1, 7, 2, 3),
    (30, 0, 2, 6, 5, 1), (30, 0, 2, 14, 5, 0), (31, 0, 4, 5, 7, 6), (35, 0, 8, 10, 3, 2), (35, 0, 8, 9, 7, 6), (37, 0, 8, 10, 0, 2),
    (38, 0, 2, 14, 4, 0), (38, 1, 0, 2, 1, 4), (38, 0, 2, 6, 4, 1), (38, 0, 2, 3, 7, 6), (40, 0, 8, 9, 6, 6), (41, 0, 2, 6, 1, 1),
    (41, 0, 2, 14, 1, 0), (42, 0, 2, 14, 2, 0), (42, 0, 2, 6, 2, 1), (42, 0, 2, 3, 6, 6), (43, 1, 7, 5, 0, 3), (47, 1, 3, 5, 2, 4),
    (53, 1, 1, 7, 3, 3), (53, 1, 1, 3, 3, 4), (55, 0, 6, 10, 5, 1), (57, 0, 14, 10, 4, 0), (60, 1, 0, 6, 3, 3), (60, 0, 6, 7, 7, 6),
    (61, 0, 14, 10, 1, 0), (62, 0, 14, 15, 7, 6), (67, 0, 6, 10, 2, 1), (70, 0, 14, 15, 6, 6), (72, 0, 6, 7, 6, 6), (74, 1, 3, 5, 3, 4),
    (78, 0, 10, 11, 7, 6), (83, 0, 10, 11, 6, 6),
)
TARGETS = ("y+", "y-", "zl", "x+", "x-", "zh", "sib")


def make_plan():
    when_a, when_b, triggers = [0] * 32, [0] * 32, [NOTHING] * (len(ORDER) + 1)
    for n, (kind, slot, piece) in enumerate(ORDER, 1):
        if kind == 0:
            when_a[slot * 2 + A_HALF[piece]] = n
        else:
            when_b[slot * 4 + piece] = n
            triggers[n] = 32 + slot * 4 + piece
    for at in range(2, 32):
        triggers[when_a[at]] = at
    for at in range(2):
        when_a[at] = triggers.index(NOTHING, 1)
        triggers[when_a[at]] = at
    return when_a, when_b, triggers


NOTHING = 127
OWN = 10
WHEN_A, WHEN_B, TRIGGERS = make_plan()
LENGTHS = [(B_PIECES if copy[1] else A_PIECES)[copy[4]][1] for copy in COPIES]
SENT = [sorted(range(len(COPIES)), key=lambda i: (LENGTHS[i], i)).index(n) for n in range(len(COPIES))]


def kernel(a_hbm, b_hbm, rows_hbm, cols_hbm, screen_hbm, keep_hbm, owners_hbm, out, a_rows, b_cols, screen, keep, owners, a_in, b_in, a_all, b_all, total, dense, stage, lists, meta_a,
           meta_b, owned_m, owned_f, a_recv, b_recv, sent, ma_send, ma_recv, mb_send, mb_recv, out_send, out_recv, own_sem, in_sem):
    row, col = lax.axis_index("row"), lax.axis_index("col")
    rem, div = lax.rem, lax.div
    x, zh = div(row, 2), rem(row, 2)
    y, zl, core = div(col, 4), rem(div(col, 2), 2), rem(col, 2)
    targets = {
        "y+": (row, rem(col + 4, 16)),
        "y-": (row, rem(col + 12, 16)),
        "zl": (row, col + 2 - 4 * zl),
        "sib": (row, col + 1 - 2 * core),
        "x+": (rem(row + 2, 8), col),
        "x-": (rem(row + 6, 8), col),
        "zh": (row + 1 - 2 * zh, col),
    }

    barrier = pltpu.get_barrier_semaphore()

    @pl.loop(1, 16)
    def _(t):
        pl.semaphore_signal(barrier, inc=1, device_id=(row, rem(col + t, 16)), device_id_type=MESH)

    @pl.loop(1, 8)
    def _(t):
        pl.semaphore_signal(barrier, inc=1, device_id=(rem(row + t, 8), col), device_id_type=MESH)

    loads = [
        pltpu.make_async_copy(source, there, in_sem.at[i]) for i, (source, there) in enumerate((
            (rows_hbm, a_rows), (cols_hbm, b_cols), (a_hbm, a_in), (b_hbm, b_in), (screen_hbm, screen), (keep_hbm, keep),
            (owners_hbm, owners)))]
    for load in loads:
        load.start()
    loads[0].wait()
    loads[1].wait()

    def note(at, value):
        lists[at] = value
        meta_a[col, at] = value
        meta_b[row, at] = value

    for i in list(range(36, 64)) + list(range(104, W)):
        lists[i] = I32(0)
    for k in range(4):
        gone = I32(28)
        places = [I32(0)] * 8
        for a in range(7):
            at = a_rows[k, a]
            gone = gone - at
            places = [jnp.where(at == r, a, v) for r, v in enumerate(places)]
        for r in range(8):
            note(k * 8 + r, places[r])
        note(32 + k, gone)
    for h in range(2):
        for k in range(4):
            gone = I32(6)
            places = [I32(0)] * 4
            for b in range(3):
                at = b_cols[b, h, k]
                gone = gone - at
                places = [jnp.where(at == c, b, v) for c, v in enumerate(places)]
            for c in range(4):
                note(64 + h * 16 + k * 4 + c, places[c])
            note(96 + h * 4 + k, gone)

    def sort_half(half):
        for k in range(2 * half, 2 * half + 2):
            gone = lists[32 + k]
            for n in range(7):
                a_all[0, k * 7 + n] = a_in[k, lists[k * 8 + n + jnp.where(n >= gone, 1, 0)]]
        if half == 0:
            loads[3].wait()
        for hk in (2 * half, 2 * half + 1, 2 * half + 4, 2 * half + 5):
            gone = lists[96 + hk]
            for n in range(3):
                b_all[0, hk * 3 + n] = b_in[hk, lists[64 + hk * 4 + n + jnp.where(n >= gone, 1, 0)]]

    loads[2].wait()
    sort_half(0)

    def copy_of(number):
        _, kind, slot, there, piece, target = COPIES[number]
        ref, pieces, recv = (b_all, B_PIECES, b_recv) if kind else (a_all, A_PIECES, a_recv)
        lo, n = pieces[piece]
        return pltpu.make_async_remote_copy(
            src_ref=ref.at[slot, pl.ds(lo, n)], dst_ref=ref.at[there, pl.ds(lo, n)],
            send_sem=sent.at[SENT[number]], recv_sem=recv.at[there * len(pieces) + piece],
            device_id=targets[TARGETS[target]], device_id_type=MESH)

    def arrival_of(kind, slot, piece):
        ref, pieces, recv = (b_all, B_PIECES, b_recv) if kind else (a_all, A_PIECES, a_recv)
        lo, n = pieces[piece]
        there = ref.at[slot, pl.ds(lo, n)]
        return pltpu.make_async_remote_copy(
            src_ref=there, dst_ref=there, send_sem=sent.at[0], recv_sem=recv.at[slot * len(pieces) + piece],
            device_id=targets["sib"], device_id_type=MESH)

    def meta_a_copy(t):
        return pltpu.make_async_remote_copy(
            src_ref=lists, dst_ref=meta_a.at[col], send_sem=ma_send.at[t], recv_sem=ma_recv.at[col],
            device_id=(row, rem(col + t, 16)), device_id_type=MESH)

    def meta_b_copy(t):
        return pltpu.make_async_remote_copy(
            src_ref=lists, dst_ref=meta_b.at[row], send_sem=mb_send.at[t], recv_sem=mb_recv.at[row],
            device_id=(rem(row + t, 8), col), device_id_type=MESH)

    def in_half(copy):
        return B_PIECES[copy[4]][0] // 6 % 2 if copy[1] else A_HALF[copy[4]]

    pl.semaphore_wait(barrier, 22)
    own = [(number, copy) for number, copy in enumerate(COPIES) if copy[0] == 0]
    first = [number for number, copy in own if in_half(copy) == 0]
    @pl.loop(1, 16)
    def _(t):
        meta_a_copy(t).start()

    @pl.loop(1, 8)
    def _(t):
        meta_b_copy(t).start()

    for number in first:
        copy_of(number).start()
    sort_half(1)
    for number, copy in own:
        if in_half(copy) == 1:
            copy_of(number).start()

    for load in loads[4:]:
        load.wait()

    @pl.loop(0, 16)
    def _(o):
        first, last = I32(32), I32(-1)
        for m in range(32):
            here = owners[m] == o
            first = jnp.where(here, jnp.minimum(first, m), first)
            last = jnp.where(here, m, last)
        some, two = last >= 0, last > first
        first = jnp.where(some, first, 0)
        last = jnp.where(two, last, 0)
        owned_m[2 * o] = rem(first, 4) * 8 + div(first, 4)
        owned_m[2 * o + 1] = rem(last, 4) * 8 + div(last, 4)
        owned_f[2 * o] = jnp.where(some, keep[first], 0).astype(F32)
        owned_f[2 * o + 1] = jnp.where(two, keep[last], 0).astype(F32)

    @pl.loop(0, 32)
    def _(m):
        total[m] = jnp.zeros((W, W), F32)

    @pl.loop(1, 16)
    def _(t):
        source = rem(col + t, 16)
        pltpu.make_async_remote_copy(
            src_ref=meta_a.at[source], dst_ref=meta_a.at[source], send_sem=ma_send.at[t], recv_sem=ma_recv.at[source],
            device_id=(row, source), device_id_type=MESH).wait_recv()

    @pl.loop(1, 8)
    def _(t):
        source = rem(row + t, 8)
        pltpu.make_async_remote_copy(
            src_ref=meta_b.at[source], dst_ref=meta_b.at[source], send_sem=mb_send.at[t], recv_sem=mb_recv.at[source],
            device_id=(source, col), device_id_type=MESH).wait_recv()

    def multiply(qa, half, qb, h, s, g, p):
        first = half * 14
        own_rows = [[meta_a[g, half * 16 + kk * 8 + r] for r in range(8)] for kk in range(2)]
        own_cols = [[meta_b[p, 64 + h * 16 + half * 8 + kk * 4 + c] for c in range(4)] for kk in range(2)]
        no_row = [meta_a[g, 32 + half * 2 + kk] for kk in range(2)]
        no_col = [meta_b[p, 96 + h * 4 + half * 2 + kk] for kk in range(2)]
        for kk in range(2):
            for r in range(8):
                low = a_all[qa, first + kk * 7 + min(r, 6)]
                high = a_all[qa, first + kk * 7 + max(r - 1, 0)]
                dense[r * W:(r + 1) * W, kk * W:(kk + 1) * W] = jnp.where(
                    r == no_row[kk], jnp.zeros_like(low), jnp.where(r < no_row[kk], low, high))
        for c in range(4):
            right = []
            for kk in range(2):
                at = h * 12 + half * 6 + kk * 3
                low = b_all[qb, at + min(c, 2)]
                high = b_all[qb, at + max(c - 1, 0)]
                right.append(jnp.where(
                    c == no_col[kk], jnp.zeros_like(low), jnp.where(c < no_col[kk], low, high)))
            rows = []
            for r in range(8):
                cells = []
                for kk in range(2):
                    passed = screen[own_rows[kk][r], own_cols[kk][c], half * 2 + kk, s].astype(F32)
                    cells.append(dense[r * W:(r + 1) * W, kk * W:(kk + 1) * W] * passed.astype(BF16))
                rows.append(jnp.concatenate(cells, axis=1))
            left = jnp.concatenate(rows, axis=0)
            part = jnp.dot(left, jnp.concatenate(right, axis=0), preferred_element_type=F32)
            total[c * 8:(c + 1) * 8] += part.reshape(8, W, W)

    def pair_of(s):
        g, e = (col + s) & 15, (row + s) & 15
        p, h = e & 7, e >> 3
        qa = 4 * (((g >> 2) - y) & 3) + 2 * (((g >> 1) & 1) ^ zl) + ((g & 1) ^ core)
        qb = 2 * (((p >> 1) - x) & 3) + ((p & 1) ^ zh)
        return g, p, h, qa, qb

    def ready_after(n):
        code = TRIGGERS[n]
        if code == NOTHING:
            return I32(-1)
        half, which = code % 2, code // 2 % 16
        if code < 32:
            g = 4 * ((y + which // 4) & 3) + 2 * (zl ^ (which // 2 % 2)) + (core ^ (which % 2))
            s = (g - col) & 15
            _, _, h, _, qb = pair_of(s)
            there = [WHEN_B[at * 2 + half] <= n for at in range(16)]
            at = 2 * qb + h
        else:
            p = 2 * ((x + which // 4) & 3) + (zh ^ (which // 2 % 2))
            s = (p + 8 * (which % 2) - row) & 15
            at = pair_of(s)[3]
            there = [WHEN_A[at * 2 + half] < n for at in range(16)]
        if not any(there):
            return I32(-1)
        both = lax.shift_right_logical(I32(sum(1 << i for i, v in enumerate(there) if v)), at) & 1
        return jnp.where(both == 1, 2 * s + half, -1)

    def receive(n, low, high):
        if high - low > 1:
            middle = (low + high) // 2
            return lax.cond(n < middle, lambda: receive(n, low, middle), lambda: receive(n, middle, high))
        arrival_of(*ORDER[low - 1]).wait_recv()
        for number, copy in enumerate(COPIES):
            if copy[0] == low:
                copy_of(number).start()
        return ready_after(low)

    @pl.loop(1, len(ORDER) + 1)
    def _(n):
        code = receive(n, 1, len(ORDER) + 1)

        @pl.when(code >= 0)
        def _():
            s, half = code >> 1, code & 1
            g, p, h, qa, qb = pair_of(s)
            multiply(qa, half, qb, h, s, g, p)

    def owner_at(u):
        dy, dz, dk = rem(2 + 3 * u, 4), 1 - div(u, 8), rem(div(u, 4), 2)
        return 4 * rem(y + dy, 4) + 2 * rem(zl + dz, 2) + rem(core + dk, 2)

    def out_copy(u):
        return pltpu.make_async_remote_copy(
            src_ref=stage.at[u], dst_ref=out.at[col], send_sem=out_send.at[u], recv_sem=out_recv.at[col],
            device_id=(row, owner_at(u)), device_id_type=MESH)

    def own_copy():
        return pltpu.make_async_copy(stage.at[OWN], out.at[col], own_sem)

    @pl.loop(0, 16)
    def _(u):
        o = owner_at(u)
        for slot in range(2):
            stage[u, slot] = (total[owned_m[2 * o + slot]] * owned_f[2 * o + slot]).astype(BF16)

        @pl.when(u != OWN)
        def _():
            out_copy(u).start()

        @pl.when(u == OWN)
        def _():
            own_copy().start()

    @pl.loop(1, 16)
    def _(t):
        meta_a_copy(t).wait_send()

    @pl.loop(1, 8)
    def _(t):
        meta_b_copy(t).wait_send()

    for length in sorted(set(LENGTHS)):
        some = [SENT[number] for number, its in enumerate(LENGTHS) if its == length]

        @pl.loop(min(some), max(some) + 1)
        def _(at, length=length):
            block = a_all.at[0, pl.ds(0, length)]
            pltpu.make_async_remote_copy(
                src_ref=block, dst_ref=block, send_sem=sent.at[at], recv_sem=a_recv.at[0],
                device_id=targets["sib"], device_id_type=MESH).wait_send()

    @pl.loop(0, 16)
    def _(u):
        @pl.when(u != OWN)
        def _():
            out_copy(u).wait_send()
            source = owner_at(u)
            pltpu.make_async_remote_copy(
                src_ref=stage.at[u], dst_ref=out.at[source], send_sem=out_send.at[u], recv_sem=out_recv.at[source],
                device_id=(row, source), device_id_type=MESH).wait_recv()

    own_copy().wait()


def on_device(a_blocks, a_rows, b_blocks, b_cols, screen, keep, owners):
    hbm = pl.BlockSpec(memory_space=pl.ANY)
    dma = pltpu.SemaphoreType.DMA
    out = pl.pallas_call(
        kernel,
        out_shape=jax.ShapeDtypeStruct((16, 2, W, W), BF16),
        in_specs=[hbm] * 7,
        out_specs=hbm,
        scratch_shapes=[
            pltpu.SMEM((4, 7), I32),
            pltpu.SMEM((3, 2, 4), I32),
            pltpu.SMEM((7, 3, 4, 16), I32),
            pltpu.SMEM((32,), I32),
            pltpu.SMEM((32,), I32),
            pltpu.VMEM((4, 7, W, W), BF16),
            pltpu.VMEM((8, 3, W, W), BF16),
            pltpu.VMEM((16, 28, W, W), BF16),
            pltpu.VMEM((8, 24, W, W), BF16),
            pltpu.VMEM((32, W, W), F32),
            pltpu.VMEM((8 * W, 2 * W), BF16),
            pltpu.VMEM((16, 2, W, W), BF16),
            pltpu.SMEM((W,), I32),
            pltpu.SMEM((16, W), I32),
            pltpu.SMEM((8, W), I32),
            pltpu.SMEM((32,), I32),
            pltpu.SMEM((32,), F32),
            dma((16 * len(A_PIECES),)),
            dma((8 * len(B_PIECES),)),
            dma((len(COPIES),)),
            dma((16,)),
            dma((16,)),
            dma((8,)),
            dma((8,)),
            dma((16,)),
            dma((16,)),
            dma,
            dma((7,)),
        ],
        compiler_params=pltpu.CompilerParams(
            collective_id=0, has_side_effects=True, vmem_limit_bytes=60 * 2**20),
        cost_estimate=pl.CostEstimate(flops=8_600_000_000, bytes_accessed=4_000_000, transcendentals=0),
        name="gather_multiply_send",
    )(
        a_blocks[0, 0], b_blocks[0, 0].reshape(8, 3, W, W), a_rows[0, 0], jnp.transpose(b_cols[0, 0], (2, 0, 1)),
        jnp.transpose(screen[0, 0], (2, 3, 1, 0)), keep[0, 0], owners[0, 0, :, 0],
    )
    return out[None, None]


def solution(mesh):
    in_specs = (
        P("row", "col", None, None, None, None),
        P("row", "col", None, None),
        P("row", "col", None, None, None, None, None),
        P("row", "col", None, None, None),
        P("row", "col", None, None, None, None),
        P("row", "col", None),
        P("row", "col", None, None),
    )
    out_specs = P("row", "col", None, None, None, None)
    return jax.shard_map(
        on_device, mesh=mesh, in_specs=in_specs, out_specs=out_specs, check_vma=False
    )
```

```python
import functools

import jax
import jax.numpy as jnp
from jax import lax
from jax.experimental import pallas as pl
from jax.experimental.pallas import tpu as pltpu
from jax.sharding import PartitionSpec as P

MESH = pl.DeviceIdType.MESH
BF16, F32, I32 = jnp.bfloat16, jnp.float32, jnp.int32
W = 128

A_PIECES = ((0, 3), (3, 5), (8, 6), (14, 3), (17, 5), (22, 6), (0, 14), (14, 14))
B_PIECES = ((0, 6), (6, 6), (12, 6), (18, 6))
A_HALF = tuple(lo // 14 for lo, _ in A_PIECES)
ORDER = (
    (0, 4, 0), (1, 1, 2), (1, 2, 3), (0, 12, 1), (1, 2, 2), (1, 6, 1), (0, 4, 1), (1, 1, 0), (1, 2, 0), (0, 12, 4),
    (0, 4, 2), (1, 4, 1), (1, 7, 2), (0, 6, 0), (0, 1, 7), (1, 1, 1), (1, 3, 2), (0, 12, 0), (0, 5, 6), (0, 2, 0),
    (0, 4, 3), (1, 6, 0), (1, 7, 0), (0, 4, 5), (0, 8, 1), (0, 2, 2), (0, 12, 2), (0, 1, 6), (1, 4, 3), (0, 12, 3),
    (0, 2, 1), (0, 8, 0), (1, 7, 1), (0, 8, 2), (0, 12, 5), (1, 4, 2), (0, 3, 6), (0, 4, 4), (1, 3, 0), (0, 9, 6),
    (1, 4, 0), (0, 13, 6), (0, 2, 5), (0, 14, 1), (0, 5, 7), (0, 6, 1), (0, 14, 2), (0, 2, 4), (0, 13, 7), (0, 6, 2),
    (1, 5, 0), (0, 8, 4), (1, 1, 3), (0, 8, 5), (0, 8, 3), (1, 5, 2), (0, 7, 6), (0, 2, 3), (0, 14, 0), (1, 3, 1),
    (1, 6, 2), (1, 2, 1), (0, 14, 5), (0, 6, 5), (0, 3, 7), (1, 5, 1), (0, 9, 7), (0, 14, 3), (0, 15, 6), (0, 6, 3),
    (0, 6, 4), (1, 3, 3), (1, 6, 3), (0, 10, 0), (0, 14, 4), (0, 10, 2), (0, 7, 7), (0, 10, 1), (1, 7, 3), (0, 15, 7),
    (0, 10, 3), (0, 10, 5), (0, 10, 4), (0, 11, 6), (1, 5, 3), (0, 11, 7),
)
COPIES = (
    (0, 0, 0, 12, 1, 0), (0, 0, 0, 4, 0, 1), (0, 1, 0, 1, 2, 5), (0, 1, 0, 2, 2, 4), (0, 0, 0, 12, 0, 0), (0, 1, 0, 6, 1, 3),
    (0, 1, 0, 2, 3, 4), (0, 0, 0, 4, 2, 1), (0, 0, 0, 12, 5, 0), (0, 0, 0, 1, 7, 6), (0, 0, 0, 4, 1, 1), (0, 0, 0, 4, 4, 1),
    (0, 0, 0, 2, 0, 2), (0, 1, 0, 1, 0, 5), (1, 1, 0, 6, 0, 3), (1, 1, 0, 1, 1, 5), (1, 0, 0, 4, 5, 1), (1, 0, 4, 6, 0, 2),
    (1, 1, 0, 2, 0, 4), (2, 1, 1, 7, 2, 3), (2, 1, 1, 3, 2, 4), (2, 0, 0, 12, 4, 0), (3, 0, 0, 1, 6, 6), (3, 0, 0, 12, 2, 0),
    (3, 1, 2, 4, 3, 4), (4, 0, 12, 8, 1, 0), (4, 0, 0, 2, 2, 2), (4, 0, 0, 4, 3, 1), (5, 1, 2, 4, 2, 4), (6, 0, 0, 12, 3, 0),
    (6, 1, 6, 4, 1, 3), (8, 1, 1, 3, 0, 4), (8, 1, 1, 7, 0, 3), (9, 0, 0, 2, 1, 2), (11, 0, 0, 2, 5, 2), (11, 0, 4, 8, 2, 1),
    (11, 0, 4, 5, 6, 6), (12, 0, 0, 2, 4, 2), (14, 1, 0, 1, 3, 5), (16, 1, 1, 3, 1, 4), (16, 1, 1, 7, 1, 3), (17, 1, 3, 5, 2, 4),
    (17, 0, 0, 2, 3, 2), (18, 0, 12, 14, 0, 2), (18, 0, 12, 8, 0, 0), (21, 0, 4, 6, 3, 2), (21, 0, 4, 8, 3, 1), (22, 1, 6, 4, 0, 3),
    (23, 1, 7, 5, 0, 3), (26, 0, 2, 6, 2, 1), (26, 0, 2, 14, 2, 0), (27, 1, 0, 6, 2, 3), (27, 0, 12, 13, 6, 6), (30, 0, 12, 14, 3, 2),
    (31, 0, 2, 6, 1, 1), (31, 0, 2, 14, 1, 0), (31, 0, 2, 3, 6, 6), (32, 0, 8, 10, 0, 2), (33, 1, 7, 5, 1, 3), (34, 0, 8, 9, 6, 6),
    (35, 0, 12, 8, 5, 0), (35, 0, 12, 13, 7, 6), (38, 0, 4, 8, 4, 1), (38, 0, 4, 5, 7, 6), (43, 0, 2, 6, 5, 1), (43, 0, 2, 14, 5, 0),
    (44, 0, 14, 10, 1, 0), (47, 1, 0, 2, 1, 4), (48, 0, 2, 14, 4, 0), (48, 0, 2, 6, 4, 1), (49, 1, 0, 6, 3, 3), (50, 0, 6, 10, 2, 1),
    (50, 0, 6, 7, 6, 6), (53, 1, 1, 3, 3, 4), (53, 1, 1, 7, 3, 3), (55, 0, 8, 10, 3, 2), (55, 0, 8, 9, 7, 6), (58, 0, 2, 3, 7, 6),
    (59, 0, 14, 15, 6, 6), (63, 0, 14, 10, 5, 0), (71, 0, 6, 10, 4, 1), (71, 0, 6, 7, 7, 6), (72, 1, 3, 5, 3, 4), (75, 0, 14, 15, 7, 6),
    (78, 0, 10, 11, 6, 6), (83, 0, 10, 11, 7, 6),
)
TARGETS = ("y+", "y-", "zl", "x+", "x-", "zh", "sib")


def make_plan():
    when_a, when_b, triggers = [0] * 32, [0] * 32, [NOTHING] * (len(ORDER) + 1)
    for n, (kind, slot, piece) in enumerate(ORDER, 1):
        if kind == 0:
            when_a[slot * 2 + A_HALF[piece]] = n
        else:
            when_b[slot * 4 + piece] = n
            triggers[n] = 32 + slot * 4 + piece
    for at in range(2, 32):
        triggers[when_a[at]] = at
    for at in range(2):
        when_a[at] = triggers.index(NOTHING, 1)
        triggers[when_a[at]] = at
    return when_a, when_b, triggers


NOTHING = 127
OWN = 10
WHEN_A, WHEN_B, TRIGGERS = make_plan()


def partners(n):
    code = TRIGGERS[n]
    if code == NOTHING:
        return ()
    half = code % 2
    there = [WHEN_B[at * 2 + half] <= n if code < 32 else WHEN_A[at * 2 + half] < n for at in range(16)]
    return there if any(there) else ()


def make_groups():
    groups = [[]]
    for n in range(1, len(ORDER) + 1):
        groups[-1].append(n)
        if partners(n) and n < len(ORDER):
            groups.append([])
    return groups


GROUPS = make_groups()
LENGTHS = [(B_PIECES if copy[1] else A_PIECES)[copy[4]][1] for copy in COPIES]
SENT = [sorted(range(len(COPIES)), key=lambda i: (LENGTHS[i], i)).index(n) for n in range(len(COPIES))]


def kernel(a_hbm, b_hbm, rows_hbm, cols_hbm, screen_hbm, keep_hbm, owners_hbm, out, a_rows, b_cols, screen, keep, owners, a_in, b_in, a_all, b_all, total, dense, stage, lists, meta_a,
           meta_b, owned_m, owned_f, a_recv, b_recv, sent, ma_send, ma_recv, mb_send, mb_recv, out_send, out_recv, own_sem, in_sem):
    row, col = lax.axis_index("row"), lax.axis_index("col")
    rem, div = lax.rem, lax.div
    x, zh = div(row, 2), rem(row, 2)
    y, zl, core = div(col, 4), rem(div(col, 2), 2), rem(col, 2)
    targets = {
        "y+": (row, rem(col + 4, 16)),
        "y-": (row, rem(col + 12, 16)),
        "zl": (row, col + 2 - 4 * zl),
        "sib": (row, col + 1 - 2 * core),
        "x+": (rem(row + 2, 8), col),
        "x-": (rem(row + 6, 8), col),
        "zh": (row + 1 - 2 * zh, col),
    }

    barrier = pltpu.get_barrier_semaphore()

    @pl.loop(1, 16)
    def _(t):
        pl.semaphore_signal(barrier, inc=1, device_id=(row, rem(col + t, 16)), device_id_type=MESH)

    @pl.loop(1, 8)
    def _(t):
        pl.semaphore_signal(barrier, inc=1, device_id=(rem(row + t, 8), col), device_id_type=MESH)

    loads = [
        pltpu.make_async_copy(source, there, in_sem.at[i]) for i, (source, there) in enumerate((
            (rows_hbm, a_rows), (cols_hbm, b_cols), (a_hbm, a_in), (b_hbm, b_in), (screen_hbm, screen), (keep_hbm, keep),
            (owners_hbm, owners)))]
    for load in loads:
        load.start()
    loads[0].wait()
    loads[1].wait()

    def note(at, value):
        lists[at] = value
        meta_a[col, at] = value
        meta_b[row, at] = value

    for i in list(range(36, 64)) + list(range(104, W)):
        lists[i] = I32(0)
    for k in range(4):
        gone = I32(28)
        places = [I32(0)] * 8
        for a in range(7):
            at = a_rows[k, a]
            gone = gone - at
            places = [jnp.where(at == r, a, v) for r, v in enumerate(places)]
        for r in range(8):
            note(k * 8 + r, places[r])
        note(32 + k, gone)
    for h in range(2):
        for k in range(4):
            gone = I32(6)
            places = [I32(0)] * 4
            for b in range(3):
                at = b_cols[b, h, k]
                gone = gone - at
                places = [jnp.where(at == c, b, v) for c, v in enumerate(places)]
            for c in range(4):
                note(64 + h * 16 + k * 4 + c, places[c])
            note(96 + h * 4 + k, gone)

    def sort_half(half):
        for k in range(2 * half, 2 * half + 2):
            gone = lists[32 + k]
            for n in range(7):
                a_all[0, k * 7 + n] = a_in[k, lists[k * 8 + n + jnp.where(n >= gone, 1, 0)]]
        if half == 0:
            loads[3].wait()
        for hk in (2 * half, 2 * half + 1, 2 * half + 4, 2 * half + 5):
            gone = lists[96 + hk]
            for n in range(3):
                b_all[0, hk * 3 + n] = b_in[hk, lists[64 + hk * 4 + n + jnp.where(n >= gone, 1, 0)]]

    loads[2].wait()
    sort_half(0)

    def copy_of(number):
        _, kind, slot, there, piece, target = COPIES[number]
        ref, pieces, recv = (b_all, B_PIECES, b_recv) if kind else (a_all, A_PIECES, a_recv)
        lo, n = pieces[piece]
        return pltpu.make_async_remote_copy(
            src_ref=ref.at[slot, pl.ds(lo, n)], dst_ref=ref.at[there, pl.ds(lo, n)],
            send_sem=sent.at[SENT[number]], recv_sem=recv.at[there * len(pieces) + piece],
            device_id=targets[TARGETS[target]], device_id_type=MESH)

    def arrival_of(kind, slot, piece):
        ref, pieces, recv = (b_all, B_PIECES, b_recv) if kind else (a_all, A_PIECES, a_recv)
        lo, n = pieces[piece]
        there = ref.at[slot, pl.ds(lo, n)]
        return pltpu.make_async_remote_copy(
            src_ref=there, dst_ref=there, send_sem=sent.at[0], recv_sem=recv.at[slot * len(pieces) + piece],
            device_id=targets["sib"], device_id_type=MESH)

    def meta_a_copy(t):
        return pltpu.make_async_remote_copy(
            src_ref=lists, dst_ref=meta_a.at[col], send_sem=ma_send.at[t], recv_sem=ma_recv.at[col],
            device_id=(row, rem(col + t, 16)), device_id_type=MESH)

    def meta_b_copy(t):
        return pltpu.make_async_remote_copy(
            src_ref=lists, dst_ref=meta_b.at[row], send_sem=mb_send.at[t], recv_sem=mb_recv.at[row],
            device_id=(rem(row + t, 8), col), device_id_type=MESH)

    def in_half(copy):
        return B_PIECES[copy[4]][0] // 6 % 2 if copy[1] else A_HALF[copy[4]]

    pl.semaphore_wait(barrier, 22)
    own = [(number, copy) for number, copy in enumerate(COPIES) if copy[0] == 0]
    first = [number for number, copy in own if in_half(copy) == 0]
    @pl.loop(1, 16)
    def _(t):
        meta_a_copy(t).start()

    @pl.loop(1, 8)
    def _(t):
        meta_b_copy(t).start()

    for number in first:
        copy_of(number).start()
    sort_half(1)
    for number, copy in own:
        if in_half(copy) == 1:
            copy_of(number).start()

    for load in loads[4:]:
        load.wait()

    @pl.loop(0, 16)
    def _(o):
        first, last = I32(32), I32(-1)
        for m in range(32):
            here = owners[m] == o
            first = jnp.where(here, jnp.minimum(first, m), first)
            last = jnp.where(here, m, last)
        some, two = last >= 0, last > first
        first = jnp.where(some, first, 0)
        last = jnp.where(two, last, 0)
        owned_m[2 * o] = rem(first, 4) * 8 + div(first, 4)
        owned_m[2 * o + 1] = rem(last, 4) * 8 + div(last, 4)
        owned_f[2 * o] = jnp.where(some, keep[first], 0).astype(F32)
        owned_f[2 * o + 1] = jnp.where(two, keep[last], 0).astype(F32)

    @pl.loop(0, 32)
    def _(m):
        total[m] = jnp.zeros((W, W), F32)

    @pl.loop(1, 16)
    def _(t):
        source = rem(col + t, 16)
        pltpu.make_async_remote_copy(
            src_ref=meta_a.at[source], dst_ref=meta_a.at[source], send_sem=ma_send.at[t], recv_sem=ma_recv.at[source],
            device_id=(row, source), device_id_type=MESH).wait_recv()

    @pl.loop(1, 8)
    def _(t):
        source = rem(row + t, 8)
        pltpu.make_async_remote_copy(
            src_ref=meta_b.at[source], dst_ref=meta_b.at[source], send_sem=mb_send.at[t], recv_sem=mb_recv.at[source],
            device_id=(source, col), device_id_type=MESH).wait_recv()

    def multiply(qa, half, qb, h, s, g, p):
        first = half * 14
        own_rows = [[meta_a[g, half * 16 + kk * 8 + r] for r in range(8)] for kk in range(2)]
        own_cols = [[meta_b[p, 64 + h * 16 + half * 8 + kk * 4 + c] for c in range(4)] for kk in range(2)]
        no_row = [meta_a[g, 32 + half * 2 + kk] for kk in range(2)]
        no_col = [meta_b[p, 96 + h * 4 + half * 2 + kk] for kk in range(2)]
        for kk in range(2):
            at = h * 12 + half * 6 + kk * 3
            for c in range(4):
                low = b_all[qb, at + min(c, 2)]
                high = b_all[qb, at + max(c - 1, 0)]
                dense[kk * W:(kk + 1) * W, c * W:(c + 1) * W] = jnp.where(
                    c == no_col[kk], jnp.zeros_like(low), jnp.where(c < no_col[kk], low, high))
        for r in range(8):
            left, right = [], []
            for kk in range(2):
                low = a_all[qa, first + kk * 7 + min(r, 6)]
                high = a_all[qa, first + kk * 7 + max(r - 1, 0)]
                left.append(jnp.where(
                    r == no_row[kk], jnp.zeros_like(low), jnp.where(r < no_row[kk], low, high)))
                cells = []
                for c in range(4):
                    passed = screen[own_rows[kk][r], own_cols[kk][c], half * 2 + kk, s].astype(F32)
                    cells.append(dense[kk * W:(kk + 1) * W, c * W:(c + 1) * W] * passed.astype(BF16))
                right.append(jnp.concatenate(cells, axis=1))
            part = jnp.dot(
                jnp.concatenate(left, axis=1), jnp.concatenate(right, axis=0), preferred_element_type=F32)
            for c in range(4):
                total[c * 8 + r] += part[:, c * W:(c + 1) * W]

    def pair_of(s):
        g, e = (col + s) & 15, (row + s) & 15
        p, h = e & 7, e >> 3
        qa = 4 * (((g >> 2) - y) & 3) + 2 * (((g >> 1) & 1) ^ zl) + ((g & 1) ^ core)
        qb = 2 * (((p >> 1) - x) & 3) + ((p & 1) ^ zh)
        return g, p, h, qa, qb

    def ready_after(n):
        code = TRIGGERS[n]
        half, which, there = code % 2, code // 2 % 16, partners(n)
        if code < 32:
            g = 4 * ((y + which // 4) & 3) + 2 * (zl ^ (which // 2 % 2)) + (core ^ (which % 2))
            s = (g - col) & 15
            _, _, h, _, qb = pair_of(s)
            at = 2 * qb + h
        else:
            p = 2 * ((x + which // 4) & 3) + (zh ^ (which // 2 % 2))
            s = (p + 8 * (which % 2) - row) & 15
            at = pair_of(s)[3]
        both = lax.shift_right_logical(I32(sum(1 << i for i, v in enumerate(there) if v)), at) & 1
        return jnp.where(both == 1, 2 * s + half, -1)

    def receive(n, low, high):
        if high - low > 1:
            middle = (low + high) // 2
            return lax.cond(n < middle, lambda: receive(n, low, middle), lambda: receive(n, middle, high))
        for arrival in GROUPS[low]:
            arrival_of(*ORDER[arrival - 1]).wait_recv()
            for number, copy in enumerate(COPIES):
                if copy[0] == arrival:
                    copy_of(number).start()
        return ready_after(arrival) if partners(arrival) else I32(-1)

    @pl.loop(0, len(GROUPS))
    def _(n):
        code = receive(n, 0, len(GROUPS))

        @pl.when(code >= 0)
        def _():
            s, half = code >> 1, code & 1
            g, p, h, qa, qb = pair_of(s)
            multiply(qa, half, qb, h, s, g, p)

    def owner_at(u):
        dy, dz, dk = rem(2 + 3 * u, 4), 1 - div(u, 8), rem(div(u, 4), 2)
        return 4 * rem(y + dy, 4) + 2 * rem(zl + dz, 2) + rem(core + dk, 2)

    def out_copy(u):
        return pltpu.make_async_remote_copy(
            src_ref=stage.at[u], dst_ref=out.at[col], send_sem=out_send.at[u], recv_sem=out_recv.at[col],
            device_id=(row, owner_at(u)), device_id_type=MESH)

    def own_copy():
        return pltpu.make_async_copy(stage.at[OWN], out.at[col], own_sem)

    @pl.loop(0, 16)
    def _(u):
        o = owner_at(u)
        for slot in range(2):
            stage[u, slot] = (total[owned_m[2 * o + slot]] * owned_f[2 * o + slot]).astype(BF16)

        @pl.when(u != OWN)
        def _():
            out_copy(u).start()

        @pl.when(u == OWN)
        def _():
            own_copy().start()

    @pl.loop(1, 16)
    def _(t):
        meta_a_copy(t).wait_send()

    @pl.loop(1, 8)
    def _(t):
        meta_b_copy(t).wait_send()

    for length in sorted(set(LENGTHS)):
        some = [SENT[number] for number, its in enumerate(LENGTHS) if its == length]

        @pl.loop(min(some), max(some) + 1)
        def _(at, length=length):
            block = a_all.at[0, pl.ds(0, length)]
            pltpu.make_async_remote_copy(
                src_ref=block, dst_ref=block, send_sem=sent.at[at], recv_sem=a_recv.at[0],
                device_id=targets["sib"], device_id_type=MESH).wait_send()

    @pl.loop(0, 16)
    def _(u):
        @pl.when(u != OWN)
        def _():
            out_copy(u).wait_send()
            source = owner_at(u)
            pltpu.make_async_remote_copy(
                src_ref=stage.at[u], dst_ref=out.at[source], send_sem=out_send.at[u], recv_sem=out_recv.at[source],
                device_id=(row, source), device_id_type=MESH).wait_recv()

    own_copy().wait()


def on_device(a_blocks, a_rows, b_blocks, b_cols, screen, keep, owners):
    hbm = pl.BlockSpec(memory_space=pl.ANY)
    dma = pltpu.SemaphoreType.DMA
    out = pl.pallas_call(
        kernel,
        out_shape=jax.ShapeDtypeStruct((16, 2, W, W), BF16),
        in_specs=[hbm] * 7,
        out_specs=hbm,
        scratch_shapes=[
            pltpu.SMEM((4, 7), I32),
            pltpu.SMEM((3, 2, 4), I32),
            pltpu.SMEM((7, 3, 4, 16), I32),
            pltpu.SMEM((32,), I32),
            pltpu.SMEM((32,), I32),
            pltpu.VMEM((4, 7, W, W), BF16),
            pltpu.VMEM((8, 3, W, W), BF16),
            pltpu.VMEM((16, 28, W, W), BF16),
            pltpu.VMEM((8, 24, W, W), BF16),
            pltpu.VMEM((32, W, W), F32),
            pltpu.VMEM((2 * W, 4 * W), BF16),
            pltpu.VMEM((16, 2, W, W), BF16),
            pltpu.SMEM((W,), I32),
            pltpu.SMEM((16, W), I32),
            pltpu.SMEM((8, W), I32),
            pltpu.SMEM((32,), I32),
            pltpu.SMEM((32,), F32),
            dma((16 * len(A_PIECES),)),
            dma((8 * len(B_PIECES),)),
            dma((len(COPIES),)),
            dma((16,)),
            dma((16,)),
            dma((8,)),
            dma((8,)),
            dma((16,)),
            dma((16,)),
            dma,
            dma((7,)),
        ],
        compiler_params=pltpu.CompilerParams(
            collective_id=0, has_side_effects=True, vmem_limit_bytes=60 * 2**20),
        cost_estimate=pl.CostEstimate(flops=8_600_000_000, bytes_accessed=4_000_000, transcendentals=0),
        name="gather_multiply_send",
    )(
        a_blocks[0, 0], b_blocks[0, 0].reshape(8, 3, W, W), a_rows[0, 0], jnp.transpose(b_cols[0, 0], (2, 0, 1)),
        jnp.transpose(screen[0, 0], (2, 3, 1, 0)), keep[0, 0], owners[0, 0, :, 0],
    )
    return out[None, None]


def solution(mesh):
    in_specs = (
        P("row", "col", None, None, None, None),
        P("row", "col", None, None),
        P("row", "col", None, None, None, None, None),
        P("row", "col", None, None, None),
        P("row", "col", None, None, None, None),
        P("row", "col", None),
        P("row", "col", None, None),
    )
    out_specs = P("row", "col", None, None, None, None)
    return jax.shard_map(
        on_device, mesh=mesh, in_specs=in_specs, out_specs=out_specs, check_vma=False
    )
```

```python
import functools

import jax
import jax.numpy as jnp
from jax import lax
from jax.experimental import pallas as pl
from jax.experimental.pallas import tpu as pltpu
from jax.sharding import PartitionSpec as P

MESH = pl.DeviceIdType.MESH
BF16, F32, I32 = jnp.bfloat16, jnp.float32, jnp.int32
W = 128

A_PIECES = ((0, 3), (3, 5), (8, 6), (14, 3), (17, 5), (22, 6), (0, 14), (14, 14))
B_PIECES = ((0, 6), (6, 6), (12, 6), (18, 6))
A_HALF = tuple(lo // 14 for lo, _ in A_PIECES)
ORDER = (
    (0, 4, 0), (1, 1, 2), (1, 2, 3), (0, 12, 1), (1, 2, 2), (1, 6, 1), (0, 4, 1), (1, 1, 0), (1, 2, 0), (0, 12, 4),
    (0, 4, 2), (1, 4, 1), (1, 7, 2), (0, 6, 0), (0, 1, 7), (1, 1, 1), (1, 3, 2), (0, 12, 0), (0, 5, 6), (0, 2, 0),
    (0, 4, 3), (1, 6, 0), (1, 7, 0), (0, 4, 5), (0, 8, 1), (0, 2, 2), (0, 12, 2), (0, 1, 6), (1, 4, 3), (0, 12, 3),
    (0, 2, 1), (0, 8, 0), (1, 7, 1), (0, 8, 2), (0, 12, 5), (1, 4, 2), (0, 3, 6), (0, 4, 4), (1, 3, 0), (0, 9, 6),
    (1, 4, 0), (0, 13, 6), (0, 2, 5), (0, 14, 1), (0, 5, 7), (0, 6, 1), (0, 14, 2), (0, 2, 4), (0, 13, 7), (0, 6, 2),
    (1, 5, 0), (0, 8, 4), (1, 1, 3), (0, 8, 5), (0, 8, 3), (1, 5, 2), (0, 7, 6), (0, 2, 3), (0, 14, 0), (1, 3, 1),
    (1, 6, 2), (1, 2, 1), (0, 14, 5), (0, 6, 5), (0, 3, 7), (1, 5, 1), (0, 9, 7), (0, 14, 3), (0, 15, 6), (0, 6, 3),
    (0, 6, 4), (1, 3, 3), (1, 6, 3), (0, 10, 0), (0, 14, 4), (0, 10, 2), (0, 7, 7), (0, 10, 1), (1, 7, 3), (0, 15, 7),
    (0, 10, 3), (0, 10, 5), (0, 10, 4), (0, 11, 6), (1, 5, 3), (0, 11, 7),
)
COPIES = (
    (0, 0, 0, 12, 1, 0), (0, 0, 0, 4, 0, 1), (0, 1, 0, 1, 2, 5), (0, 1, 0, 2, 2, 4), (0, 0, 0, 12, 0, 0), (0, 1, 0, 6, 1, 3),
    (0, 1, 0, 2, 3, 4), (0, 0, 0, 4, 2, 1), (0, 0, 0, 12, 5, 0), (0, 0, 0, 1, 7, 6), (0, 0, 0, 4, 1, 1), (0, 0, 0, 4, 4, 1),
    (0, 0, 0, 2, 0, 2), (0, 1, 0, 1, 0, 5), (1, 1, 0, 6, 0, 3), (1, 1, 0, 1, 1, 5), (1, 0, 0, 4, 5, 1), (1, 0, 4, 6, 0, 2),
    (1, 1, 0, 2, 0, 4), (2, 1, 1, 7, 2, 3), (2, 1, 1, 3, 2, 4), (2, 0, 0, 12, 4, 0), (3, 0, 0, 1, 6, 6), (3, 0, 0, 12, 2, 0),
    (3, 1, 2, 4, 3, 4), (4, 0, 12, 8, 1, 0), (4, 0, 0, 2, 2, 2), (4, 0, 0, 4, 3, 1), (5, 1, 2, 4, 2, 4), (6, 0, 0, 12, 3, 0),
    (6, 1, 6, 4, 1, 3), (8, 1, 1, 3, 0, 4), (8, 1, 1, 7, 0, 3), (9, 0, 0, 2, 1, 2), (11, 0, 0, 2, 5, 2), (11, 0, 4, 8, 2, 1),
    (11, 0, 4, 5, 6, 6), (12, 0, 0, 2, 4, 2), (14, 1, 0, 1, 3, 5), (16, 1, 1, 3, 1, 4), (16, 1, 1, 7, 1, 3), (17, 1, 3, 5, 2, 4),
    (17, 0, 0, 2, 3, 2), (18, 0, 12, 14, 0, 2), (18, 0, 12, 8, 0, 0), (21, 0, 4, 6, 3, 2), (21, 0, 4, 8, 3, 1), (22, 1, 6, 4, 0, 3),
    (23, 1, 7, 5, 0, 3), (26, 0, 2, 6, 2, 1), (26, 0, 2, 14, 2, 0), (27, 1, 0, 6, 2, 3), (27, 0, 12, 13, 6, 6), (30, 0, 12, 14, 3, 2),
    (31, 0, 2, 6, 1, 1), (31, 0, 2, 14, 1, 0), (31, 0, 2, 3, 6, 6), (32, 0, 8, 10, 0, 2), (33, 1, 7, 5, 1, 3), (34, 0, 8, 9, 6, 6),
    (35, 0, 12, 8, 5, 0), (35, 0, 12, 13, 7, 6), (38, 0, 4, 8, 4, 1), (38, 0, 4, 5, 7, 6), (43, 0, 2, 6, 5, 1), (43, 0, 2, 14, 5, 0),
    (44, 0, 14, 10, 1, 0), (47, 1, 0, 2, 1, 4), (48, 0, 2, 14, 4, 0), (48, 0, 2, 6, 4, 1), (49, 1, 0, 6, 3, 3), (50, 0, 6, 10, 2, 1),
    (50, 0, 6, 7, 6, 6), (53, 1, 1, 3, 3, 4), (53, 1, 1, 7, 3, 3), (55, 0, 8, 10, 3, 2), (55, 0, 8, 9, 7, 6), (58, 0, 2, 3, 7, 6),
    (59, 0, 14, 15, 6, 6), (63, 0, 14, 10, 5, 0), (71, 0, 6, 10, 4, 1), (71, 0, 6, 7, 7, 6), (72, 1, 3, 5, 3, 4), (75, 0, 14, 15, 7, 6),
    (78, 0, 10, 11, 6, 6), (83, 0, 10, 11, 7, 6),
)
TARGETS = ("y+", "y-", "zl", "x+", "x-", "zh", "sib")


def make_plan():
    when_a, when_b, triggers = [0] * 32, [0] * 32, [NOTHING] * (len(ORDER) + 1)
    for n, (kind, slot, piece) in enumerate(ORDER, 1):
        if kind == 0:
            when_a[slot * 2 + A_HALF[piece]] = n
        else:
            when_b[slot * 4 + piece] = n
            triggers[n] = 32 + slot * 4 + piece
    for at in range(2, 32):
        triggers[when_a[at]] = at
    for at in range(2):
        when_a[at] = triggers.index(NOTHING, 1)
        triggers[when_a[at]] = at
    return when_a, when_b, triggers


NOTHING = 127
OWN = 10
WHEN_A, WHEN_B, TRIGGERS = make_plan()


def partners(n):
    code = TRIGGERS[n]
    if code == NOTHING:
        return ()
    half = code % 2
    there = [WHEN_B[at * 2 + half] <= n if code < 32 else WHEN_A[at * 2 + half] < n for at in range(16)]
    return there if any(there) else ()


def make_groups():
    groups = [[]]
    for n in range(1, len(ORDER) + 1):
        groups[-1].append(n)
        if partners(n) and n < len(ORDER):
            groups.append([])
    return groups


GROUPS = make_groups()
LENGTHS = [(B_PIECES if copy[1] else A_PIECES)[copy[4]][1] for copy in COPIES]
SENT = [sorted(range(len(COPIES)), key=lambda i: (LENGTHS[i], i)).index(n) for n in range(len(COPIES))]


def kernel(a_hbm, b_hbm, rows_hbm, cols_hbm, screen_hbm, keep_hbm, owners_hbm, out, a_rows, b_cols, screen, keep, owners, a_in, b_in, a_all, b_all, total, dense, stage, lists, meta_a,
           meta_b, owned_m, owned_f, a_recv, b_recv, sent, ma_send, ma_recv, mb_send, mb_recv, out_send, out_recv, own_sem, in_sem):
    row, col = lax.axis_index("row"), lax.axis_index("col")
    rem, div = lax.rem, lax.div
    x, zh = div(row, 2), rem(row, 2)
    y, zl, core = div(col, 4), rem(div(col, 2), 2), rem(col, 2)
    targets = {
        "y+": (row, rem(col + 4, 16)),
        "y-": (row, rem(col + 12, 16)),
        "zl": (row, col + 2 - 4 * zl),
        "sib": (row, col + 1 - 2 * core),
        "x+": (rem(row + 2, 8), col),
        "x-": (rem(row + 6, 8), col),
        "zh": (row + 1 - 2 * zh, col),
    }

    barrier = pltpu.get_barrier_semaphore()

    @pl.loop(1, 16, unroll=15)
    def _(t):
        pl.semaphore_signal(barrier, inc=1, device_id=(row, rem(col + t, 16)), device_id_type=MESH)

    @pl.loop(1, 8, unroll=7)
    def _(t):
        pl.semaphore_signal(barrier, inc=1, device_id=(rem(row + t, 8), col), device_id_type=MESH)

    loads = [
        pltpu.make_async_copy(source, there, in_sem.at[i]) for i, (source, there) in enumerate((
            (rows_hbm, a_rows), (cols_hbm, b_cols), (a_hbm, a_in), (b_hbm, b_in), (screen_hbm, screen), (keep_hbm, keep),
            (owners_hbm, owners)))]
    for load in loads:
        load.start()
    loads[0].wait()
    loads[1].wait()

    def note(at, value):
        lists[at] = value
        meta_a[col, at] = value
        meta_b[row, at] = value

    for i in list(range(36, 64)) + list(range(104, W)):
        lists[i] = I32(0)
    for k in range(4):
        gone = I32(28)
        places = [I32(0)] * 8
        for a in range(7):
            at = a_rows[k, a]
            gone = gone - at
            places = [jnp.where(at == r, a, v) for r, v in enumerate(places)]
        for r in range(8):
            note(k * 8 + r, places[r])
        note(32 + k, gone)
    for h in range(2):
        for k in range(4):
            gone = I32(6)
            places = [I32(0)] * 4
            for b in range(3):
                at = b_cols[b, h, k]
                gone = gone - at
                places = [jnp.where(at == c, b, v) for c, v in enumerate(places)]
            for c in range(4):
                note(64 + h * 16 + k * 4 + c, places[c])
            note(96 + h * 4 + k, gone)

    def sort_half(half):
        for k in range(2 * half, 2 * half + 2):
            gone = lists[32 + k]
            for n in range(7):
                a_all[0, k * 7 + n] = a_in[k, lists[k * 8 + n + jnp.where(n >= gone, 1, 0)]]
        if half == 0:
            loads[3].wait()
        for hk in (2 * half, 2 * half + 1, 2 * half + 4, 2 * half + 5):
            gone = lists[96 + hk]
            for n in range(3):
                b_all[0, hk * 3 + n] = b_in[hk, lists[64 + hk * 4 + n + jnp.where(n >= gone, 1, 0)]]

    loads[2].wait()
    sort_half(0)

    def copy_of(number):
        _, kind, slot, there, piece, target = COPIES[number]
        ref, pieces, recv = (b_all, B_PIECES, b_recv) if kind else (a_all, A_PIECES, a_recv)
        lo, n = pieces[piece]
        return pltpu.make_async_remote_copy(
            src_ref=ref.at[slot, pl.ds(lo, n)], dst_ref=ref.at[there, pl.ds(lo, n)],
            send_sem=sent.at[SENT[number]], recv_sem=recv.at[there * len(pieces) + piece],
            device_id=targets[TARGETS[target]], device_id_type=MESH)

    def arrival_of(kind, slot, piece):
        ref, pieces, recv = (b_all, B_PIECES, b_recv) if kind else (a_all, A_PIECES, a_recv)
        lo, n = pieces[piece]
        there = ref.at[slot, pl.ds(lo, n)]
        return pltpu.make_async_remote_copy(
            src_ref=there, dst_ref=there, send_sem=sent.at[0], recv_sem=recv.at[slot * len(pieces) + piece],
            device_id=targets["sib"], device_id_type=MESH)

    def meta_a_copy(t):
        return pltpu.make_async_remote_copy(
            src_ref=lists, dst_ref=meta_a.at[col], send_sem=ma_send.at[t], recv_sem=ma_recv.at[col],
            device_id=(row, rem(col + t, 16)), device_id_type=MESH)

    def meta_b_copy(t):
        return pltpu.make_async_remote_copy(
            src_ref=lists, dst_ref=meta_b.at[row], send_sem=mb_send.at[t], recv_sem=mb_recv.at[row],
            device_id=(rem(row + t, 8), col), device_id_type=MESH)

    def in_half(copy):
        return B_PIECES[copy[4]][0] // 6 % 2 if copy[1] else A_HALF[copy[4]]

    pl.semaphore_wait(barrier, 22)
    own = [(number, copy) for number, copy in enumerate(COPIES) if copy[0] == 0]
    first = [number for number, copy in own if in_half(copy) == 0]
    @pl.loop(1, 16, unroll=15)
    def _(t):
        meta_a_copy(t).start()

    @pl.loop(1, 8, unroll=7)
    def _(t):
        meta_b_copy(t).start()

    for number in first:
        copy_of(number).start()
    sort_half(1)
    for number, copy in own:
        if in_half(copy) == 1:
            copy_of(number).start()

    for load in loads[4:]:
        load.wait()

    @pl.loop(0, 16)
    def _(o):
        first, last = I32(32), I32(-1)
        for m in range(32):
            here = owners[m] == o
            first = jnp.where(here, jnp.minimum(first, m), first)
            last = jnp.where(here, m, last)
        some, two = last >= 0, last > first
        first = jnp.where(some, first, 0)
        last = jnp.where(two, last, 0)
        owned_m[2 * o] = rem(first, 4) * 8 + div(first, 4)
        owned_m[2 * o + 1] = rem(last, 4) * 8 + div(last, 4)
        owned_f[2 * o] = jnp.where(some, keep[first], 0).astype(F32)
        owned_f[2 * o + 1] = jnp.where(two, keep[last], 0).astype(F32)

    @pl.loop(0, 32)
    def _(m):
        total[m] = jnp.zeros((W, W), F32)

    @pl.loop(1, 16)
    def _(t):
        source = rem(col + t, 16)
        pltpu.make_async_remote_copy(
            src_ref=meta_a.at[source], dst_ref=meta_a.at[source], send_sem=ma_send.at[t], recv_sem=ma_recv.at[source],
            device_id=(row, source), device_id_type=MESH).wait_recv()

    @pl.loop(1, 8)
    def _(t):
        source = rem(row + t, 8)
        pltpu.make_async_remote_copy(
            src_ref=meta_b.at[source], dst_ref=meta_b.at[source], send_sem=mb_send.at[t], recv_sem=mb_recv.at[source],
            device_id=(source, col), device_id_type=MESH).wait_recv()

    def multiply(qa, half, qb, h, s, g, p):
        first = half * 14
        own_rows = [[meta_a[g, half * 16 + kk * 8 + r] for r in range(8)] for kk in range(2)]
        own_cols = [[meta_b[p, 64 + h * 16 + half * 8 + kk * 4 + c] for c in range(4)] for kk in range(2)]
        no_row = [meta_a[g, 32 + half * 2 + kk] for kk in range(2)]
        no_col = [meta_b[p, 96 + h * 4 + half * 2 + kk] for kk in range(2)]
        for kk in range(2):
            at = h * 12 + half * 6 + kk * 3
            for c in range(4):
                low = b_all[qb, at + min(c, 2)]
                high = b_all[qb, at + max(c - 1, 0)]
                dense[kk * W:(kk + 1) * W, c * W:(c + 1) * W] = jnp.where(
                    c == no_col[kk], jnp.zeros_like(low), jnp.where(c < no_col[kk], low, high))
        for r in range(8):
            left, right = [], []
            for kk in range(2):
                low = a_all[qa, first + kk * 7 + min(r, 6)]
                high = a_all[qa, first + kk * 7 + max(r - 1, 0)]
                left.append(jnp.where(
                    r == no_row[kk], jnp.zeros_like(low), jnp.where(r < no_row[kk], low, high)))
                cells = []
                for c in range(4):
                    passed = screen[own_rows[kk][r], own_cols[kk][c], half * 2 + kk, s].astype(F32)
                    cells.append(dense[kk * W:(kk + 1) * W, c * W:(c + 1) * W] * passed.astype(BF16))
                right.append(jnp.concatenate(cells, axis=1))
            part = jnp.dot(
                jnp.concatenate(left, axis=1), jnp.concatenate(right, axis=0), preferred_element_type=F32)
            for c in range(4):
                total[c * 8 + r] += part[:, c * W:(c + 1) * W]

    def pair_of(s):
        g, e = (col + s) & 15, (row + s) & 15
        p, h = e & 7, e >> 3
        qa = 4 * (((g >> 2) - y) & 3) + 2 * (((g >> 1) & 1) ^ zl) + ((g & 1) ^ core)
        qb = 2 * (((p >> 1) - x) & 3) + ((p & 1) ^ zh)
        return g, p, h, qa, qb

    def ready_after(n):
        code = TRIGGERS[n]
        half, which, there = code % 2, code // 2 % 16, partners(n)
        if code < 32:
            g = 4 * ((y + which // 4) & 3) + 2 * (zl ^ (which // 2 % 2)) + (core ^ (which % 2))
            s = (g - col) & 15
            _, _, h, _, qb = pair_of(s)
            at = 2 * qb + h
        else:
            p = 2 * ((x + which // 4) & 3) + (zh ^ (which // 2 % 2))
            s = (p + 8 * (which % 2) - row) & 15
            at = pair_of(s)[3]
        both = lax.shift_right_logical(I32(sum(1 << i for i, v in enumerate(there) if v)), at) & 1
        return jnp.where(both == 1, 2 * s + half, -1)

    def receive(n, low, high):
        if high - low > 1:
            middle = (low + high) // 2
            return lax.cond(n < middle, lambda: receive(n, low, middle), lambda: receive(n, middle, high))
        for arrival in GROUPS[low]:
            arrival_of(*ORDER[arrival - 1]).wait_recv()
            for number, copy in enumerate(COPIES):
                if copy[0] == arrival:
                    copy_of(number).start()
        return ready_after(arrival) if partners(arrival) else I32(-1)

    @pl.loop(0, len(GROUPS))
    def _(n):
        code = receive(n, 0, len(GROUPS))

        @pl.when(code >= 0)
        def _():
            s, half = code >> 1, code & 1
            g, p, h, qa, qb = pair_of(s)
            multiply(qa, half, qb, h, s, g, p)

    def owner_at(u):
        dy, dz, dk = rem(2 + 3 * u, 4), 1 - div(u, 8), rem(div(u, 4), 2)
        return 4 * rem(y + dy, 4) + 2 * rem(zl + dz, 2) + rem(core + dk, 2)

    def out_copy(u):
        return pltpu.make_async_remote_copy(
            src_ref=stage.at[u], dst_ref=out.at[col], send_sem=out_send.at[u], recv_sem=out_recv.at[col],
            device_id=(row, owner_at(u)), device_id_type=MESH)

    def own_copy():
        return pltpu.make_async_copy(stage.at[OWN], out.at[col], own_sem)

    @pl.loop(0, 16, unroll=4)
    def _(u):
        o = owner_at(u)
        for slot in range(2):
            stage[u, slot] = (total[owned_m[2 * o + slot]] * owned_f[2 * o + slot]).astype(BF16)

        @pl.when(u != OWN)
        def _():
            out_copy(u).start()

        @pl.when(u == OWN)
        def _():
            own_copy().start()

    @pl.loop(1, 16)
    def _(t):
        meta_a_copy(t).wait_send()

    @pl.loop(1, 8)
    def _(t):
        meta_b_copy(t).wait_send()

    for length in sorted(set(LENGTHS)):
        some = [SENT[number] for number, its in enumerate(LENGTHS) if its == length]

        @pl.loop(min(some), max(some) + 1)
        def _(at, length=length):
            block = a_all.at[0, pl.ds(0, length)]
            pltpu.make_async_remote_copy(
                src_ref=block, dst_ref=block, send_sem=sent.at[at], recv_sem=a_recv.at[0],
                device_id=targets["sib"], device_id_type=MESH).wait_send()

    @pl.loop(0, 16)
    def _(u):
        @pl.when(u != OWN)
        def _():
            out_copy(u).wait_send()
            source = owner_at(u)
            pltpu.make_async_remote_copy(
                src_ref=stage.at[u], dst_ref=out.at[source], send_sem=out_send.at[u], recv_sem=out_recv.at[source],
                device_id=(row, source), device_id_type=MESH).wait_recv()

    own_copy().wait()


def on_device(a_blocks, a_rows, b_blocks, b_cols, screen, keep, owners):
    hbm = pl.BlockSpec(memory_space=pl.ANY)
    dma = pltpu.SemaphoreType.DMA
    out = pl.pallas_call(
        kernel,
        out_shape=jax.ShapeDtypeStruct((16, 2, W, W), BF16),
        in_specs=[hbm] * 7,
        out_specs=hbm,
        scratch_shapes=[
            pltpu.SMEM((4, 7), I32),
            pltpu.SMEM((3, 2, 4), I32),
            pltpu.SMEM((7, 3, 4, 16), I32),
            pltpu.SMEM((32,), I32),
            pltpu.SMEM((32,), I32),
            pltpu.VMEM((4, 7, W, W), BF16),
            pltpu.VMEM((8, 3, W, W), BF16),
            pltpu.VMEM((16, 28, W, W), BF16),
            pltpu.VMEM((8, 24, W, W), BF16),
            pltpu.VMEM((32, W, W), F32),
            pltpu.VMEM((2 * W, 4 * W), BF16),
            pltpu.VMEM((16, 2, W, W), BF16),
            pltpu.SMEM((W,), I32),
            pltpu.SMEM((16, W), I32),
            pltpu.SMEM((8, W), I32),
            pltpu.SMEM((32,), I32),
            pltpu.SMEM((32,), F32),
            dma((16 * len(A_PIECES),)),
            dma((8 * len(B_PIECES),)),
            dma((len(COPIES),)),
            dma((16,)),
            dma((16,)),
            dma((8,)),
            dma((8,)),
            dma((16,)),
            dma((16,)),
            dma,
            dma((7,)),
        ],
        compiler_params=pltpu.CompilerParams(
            collective_id=0, has_side_effects=True, vmem_limit_bytes=60 * 2**20),
        cost_estimate=pl.CostEstimate(flops=8_600_000_000, bytes_accessed=4_000_000, transcendentals=0),
        name="gather_multiply_send",
    )(
        a_blocks[0, 0], b_blocks[0, 0].reshape(8, 3, W, W), a_rows[0, 0], jnp.transpose(b_cols[0, 0], (2, 0, 1)),
        jnp.transpose(screen[0, 0], (2, 3, 1, 0)), keep[0, 0], owners[0, 0, :, 0],
    )
    return out[None, None]


def solution(mesh):
    in_specs = (
        P("row", "col", None, None, None, None),
        P("row", "col", None, None),
        P("row", "col", None, None, None, None, None),
        P("row", "col", None, None, None),
        P("row", "col", None, None, None, None),
        P("row", "col", None),
        P("row", "col", None, None),
    )
    out_specs = P("row", "col", None, None, None, None)
    return jax.shard_map(
        on_device, mesh=mesh, in_specs=in_specs, out_specs=out_specs, check_vma=False
    )
```

```python
import functools

import jax
import jax.numpy as jnp
from jax import lax
from jax.experimental import pallas as pl
from jax.experimental.pallas import tpu as pltpu
from jax.sharding import PartitionSpec as P

MESH = pl.DeviceIdType.MESH
BF16, F32, I32 = jnp.bfloat16, jnp.float32, jnp.int32
W = 128

A_PIECES = ((0, 4), (4, 5), (9, 5), (14, 3), (17, 5), (22, 6), (0, 14), (14, 14))
B_PIECES = ((0, 6), (6, 6), (12, 6), (18, 6))
A_HALF = tuple(lo // 14 for lo, _ in A_PIECES)
ORDER = (
    (0, 1, 7), (0, 1, 6), (0, 2, 0), (0, 4, 0), (1, 2, 0), (1, 6, 0), (1, 2, 3), (1, 6, 3), (0, 12, 4), (0, 12, 1),
    (1, 1, 0), (0, 4, 1), (0, 12, 5), (1, 4, 0), (1, 6, 1), (0, 4, 5), (1, 2, 2), (0, 12, 0), (0, 12, 2), (0, 4, 3),
    (1, 2, 1), (0, 4, 4), (0, 4, 2), (1, 7, 0), (1, 4, 3), (0, 2, 2), (0, 2, 1), (1, 1, 3), (0, 12, 3), (0, 3, 6),
    (0, 5, 6), (0, 2, 4), (1, 4, 1), (0, 8, 3), (0, 8, 5), (0, 8, 4), (0, 13, 6), (1, 3, 0), (0, 5, 7), (1, 5, 0),
    (0, 8, 0), (1, 1, 1), (0, 6, 0), (0, 8, 1), (1, 4, 2), (0, 14, 0), (0, 8, 2), (0, 14, 2), (1, 3, 3), (0, 9, 7),
    (1, 7, 3), (0, 9, 6), (0, 2, 5), (0, 6, 1), (0, 14, 1), (1, 7, 1), (0, 2, 3), (0, 6, 2), (0, 14, 4), (1, 3, 1),
    (0, 15, 6), (0, 3, 7), (0, 6, 4), (1, 6, 2), (1, 1, 2), (0, 7, 6), (0, 6, 3), (0, 6, 5), (1, 5, 3), (0, 13, 7),
    (0, 14, 3), (0, 14, 5), (0, 7, 7), (0, 10, 1), (0, 10, 2), (1, 5, 1), (1, 3, 2), (0, 15, 7), (0, 10, 0), (0, 10, 3),
    (0, 10, 4), (0, 10, 5), (1, 7, 2), (0, 11, 6), (0, 11, 7), (1, 5, 2),
)
COPIES = (
    (0, 0, 0, 2, 0, 2), (0, 1, 0, 6, 3, 3), (0, 0, 0, 4, 0, 1), (0, 1, 0, 1, 3, 5), (0, 0, 0, 12, 5, 0), (0, 1, 0, 2, 0, 4),
    (0, 0, 0, 12, 0, 0), (0, 0, 0, 4, 3, 1), (0, 0, 0, 4, 2, 1), (0, 0, 0, 1, 7, 6), (0, 0, 0, 1, 6, 6), (0, 1, 0, 6, 0, 3),
    (0, 0, 0, 4, 1, 1), (0, 0, 0, 12, 4, 0), (0, 1, 0, 6, 1, 3), (0, 1, 0, 2, 3, 4), (1, 1, 0, 2, 1, 4), (2, 1, 0, 1, 0, 5),
    (2, 0, 0, 4, 5, 1), (3, 0, 0, 2, 2, 2), (4, 0, 4, 6, 0, 2), (4, 0, 0, 2, 1, 2), (5, 0, 0, 12, 1, 0), (5, 0, 0, 12, 2, 0),
    (6, 1, 6, 4, 0, 3), (7, 1, 0, 2, 2, 4), (7, 1, 2, 4, 3, 4), (9, 0, 12, 8, 4, 0), (9, 0, 0, 12, 3, 0), (9, 0, 0, 2, 4, 2),
    (10, 0, 0, 4, 4, 1), (10, 0, 12, 8, 1, 0), (11, 1, 1, 7, 0, 3), (11, 1, 1, 3, 0, 4), (15, 1, 6, 4, 1, 3), (15, 1, 0, 1, 1, 5),
    (16, 0, 4, 8, 5, 1), (17, 1, 2, 4, 2, 4), (18, 0, 12, 8, 0, 0), (18, 0, 12, 14, 0, 2), (18, 0, 0, 2, 5, 2), (19, 0, 0, 2, 3, 2),
    (19, 0, 12, 13, 6, 6), (20, 1, 0, 1, 2, 5), (20, 0, 4, 6, 3, 2), (20, 0, 4, 8, 3, 1), (22, 0, 4, 5, 7, 6), (23, 0, 4, 8, 2, 1),
    (23, 0, 4, 5, 6, 6), (24, 1, 7, 5, 0, 3), (26, 0, 2, 14, 2, 0), (26, 0, 2, 6, 2, 1), (27, 0, 2, 6, 1, 1), (27, 0, 2, 14, 1, 0),
    (27, 0, 2, 3, 6, 6), (28, 1, 1, 7, 3, 3), (28, 1, 1, 3, 3, 4), (29, 0, 12, 14, 3, 2), (29, 0, 12, 13, 7, 6), (32, 0, 2, 6, 4, 1),
    (32, 0, 2, 14, 4, 0), (34, 0, 8, 10, 3, 2), (36, 0, 8, 9, 7, 6), (41, 0, 8, 10, 0, 2), (42, 1, 1, 7, 1, 3), (42, 1, 1, 3, 1, 4),
    (43, 1, 0, 6, 2, 3), (47, 0, 8, 9, 6, 6), (49, 1, 3, 5, 3, 4), (53, 0, 2, 6, 5, 1), (53, 0, 2, 14, 5, 0), (55, 0, 14, 10, 1, 0),
    (55, 0, 14, 15, 6, 6), (56, 1, 7, 5, 1, 3), (57, 0, 2, 3, 7, 6), (58, 0, 6, 10, 2, 1), (58, 0, 6, 7, 6, 6), (59, 0, 14, 10, 4, 0),
    (65, 1, 1, 7, 2, 3), (65, 1, 1, 3, 2, 4), (68, 0, 6, 10, 5, 1), (68, 0, 6, 7, 7, 6), (72, 0, 14, 15, 7, 6), (77, 1, 3, 5, 2, 4),
    (79, 0, 10, 11, 6, 6), (82, 0, 10, 11, 7, 6),
)
TARGETS = ("y+", "y-", "zl", "x+", "x-", "zh", "sib")


def make_plan():
    when_a, when_b, triggers = [0] * 32, [0] * 32, [NOTHING] * (len(ORDER) + 1)
    for n, (kind, slot, piece) in enumerate(ORDER, 1):
        if kind == 0:
            when_a[slot * 2 + A_HALF[piece]] = n
        else:
            when_b[slot * 4 + piece] = n
            triggers[n] = 32 + slot * 4 + piece
    for at in range(2, 32):
        triggers[when_a[at]] = at
    for at in range(2):
        when_a[at] = triggers.index(NOTHING, 1)
        triggers[when_a[at]] = at
    return when_a, when_b, triggers


NOTHING = 127
OWN = 10
WHEN_A, WHEN_B, TRIGGERS = make_plan()


def partners(n):
    code = TRIGGERS[n]
    if code == NOTHING:
        return ()
    half = code % 2
    there = [WHEN_B[at * 2 + half] <= n if code < 32 else WHEN_A[at * 2 + half] < n for at in range(16)]
    return there if any(there) else ()


def make_groups():
    groups = [[]]
    for n in range(1, len(ORDER) + 1):
        groups[-1].append(n)
        if partners(n) and n < len(ORDER):
            groups.append([])
    return groups


GROUPS = make_groups()
LENGTHS = [(B_PIECES if copy[1] else A_PIECES)[copy[4]][1] for copy in COPIES]
SENT = [sorted(range(len(COPIES)), key=lambda i: (LENGTHS[i], i)).index(n) for n in range(len(COPIES))]


def kernel(a_hbm, b_hbm, rows_hbm, cols_hbm, screen_hbm, keep_hbm, owners_hbm, out, a_rows, b_cols, screen, keep, owners, a_in, b_in, a_all, b_all, total, dense, stage, lists, meta_a,
           meta_b, owned_m, owned_f, a_recv, b_recv, sent, ma_send, ma_recv, mb_send, mb_recv, out_send, out_recv, own_sem, in_sem):
    row, col = lax.axis_index("row"), lax.axis_index("col")
    rem, div = lax.rem, lax.div
    x, zh = div(row, 2), rem(row, 2)
    y, zl, core = div(col, 4), rem(div(col, 2), 2), rem(col, 2)
    targets = {
        "y+": (row, rem(col + 4, 16)),
        "y-": (row, rem(col + 12, 16)),
        "zl": (row, col + 2 - 4 * zl),
        "sib": (row, col + 1 - 2 * core),
        "x+": (rem(row + 2, 8), col),
        "x-": (rem(row + 6, 8), col),
        "zh": (row + 1 - 2 * zh, col),
    }

    barrier = pltpu.get_barrier_semaphore()

    @pl.loop(1, 16, unroll=15)
    def _(t):
        pl.semaphore_signal(barrier, inc=1, device_id=(row, rem(col + t, 16)), device_id_type=MESH)

    @pl.loop(1, 8, unroll=7)
    def _(t):
        pl.semaphore_signal(barrier, inc=1, device_id=(rem(row + t, 8), col), device_id_type=MESH)

    loads = [
        pltpu.make_async_copy(source, there, in_sem.at[i]) for i, (source, there) in enumerate((
            (rows_hbm, a_rows), (cols_hbm, b_cols), (a_hbm, a_in), (b_hbm, b_in), (screen_hbm, screen), (keep_hbm, keep),
            (owners_hbm, owners)))]
    for load in loads:
        load.start()
    loads[0].wait()
    loads[1].wait()

    def note(at, value):
        lists[at] = value
        meta_a[col, at] = value
        meta_b[row, at] = value

    for i in list(range(36, 64)) + list(range(104, W)):
        lists[i] = I32(0)
    for k in range(4):
        gone = I32(28)
        places = [I32(0)] * 8
        for a in range(7):
            at = a_rows[k, a]
            gone = gone - at
            places = [jnp.where(at == r, a, v) for r, v in enumerate(places)]
        for r in range(8):
            note(k * 8 + r, places[r])
        note(32 + k, gone)
    for h in range(2):
        for k in range(4):
            gone = I32(6)
            places = [I32(0)] * 4
            for b in range(3):
                at = b_cols[b, h, k]
                gone = gone - at
                places = [jnp.where(at == c, b, v) for c, v in enumerate(places)]
            for c in range(4):
                note(64 + h * 16 + k * 4 + c, places[c])
            note(96 + h * 4 + k, gone)

    def sort_half(half):
        for k in range(2 * half, 2 * half + 2):
            gone = lists[32 + k]
            for n in range(7):
                a_all[0, k * 7 + n] = a_in[k, lists[k * 8 + n + jnp.where(n >= gone, 1, 0)]]
        if half == 0:
            loads[3].wait()
        for hk in (2 * half, 2 * half + 1, 2 * half + 4, 2 * half + 5):
            gone = lists[96 + hk]
            for n in range(3):
                b_all[0, hk * 3 + n] = b_in[hk, lists[64 + hk * 4 + n + jnp.where(n >= gone, 1, 0)]]

    loads[2].wait()
    sort_half(0)

    def copy_of(number):
        _, kind, slot, there, piece, target = COPIES[number]
        ref, pieces, recv = (b_all, B_PIECES, b_recv) if kind else (a_all, A_PIECES, a_recv)
        lo, n = pieces[piece]
        return pltpu.make_async_remote_copy(
            src_ref=ref.at[slot, pl.ds(lo, n)], dst_ref=ref.at[there, pl.ds(lo, n)],
            send_sem=sent.at[SENT[number]], recv_sem=recv.at[there * len(pieces) + piece],
            device_id=targets[TARGETS[target]], device_id_type=MESH)

    def arrival_of(kind, slot, piece):
        ref, pieces, recv = (b_all, B_PIECES, b_recv) if kind else (a_all, A_PIECES, a_recv)
        lo, n = pieces[piece]
        there = ref.at[slot, pl.ds(lo, n)]
        return pltpu.make_async_remote_copy(
            src_ref=there, dst_ref=there, send_sem=sent.at[0], recv_sem=recv.at[slot * len(pieces) + piece],
            device_id=targets["sib"], device_id_type=MESH)

    def meta_a_copy(t):
        return pltpu.make_async_remote_copy(
            src_ref=lists, dst_ref=meta_a.at[col], send_sem=ma_send.at[t], recv_sem=ma_recv.at[col],
            device_id=(row, rem(col + t, 16)), device_id_type=MESH)

    def meta_b_copy(t):
        return pltpu.make_async_remote_copy(
            src_ref=lists, dst_ref=meta_b.at[row], send_sem=mb_send.at[t], recv_sem=mb_recv.at[row],
            device_id=(rem(row + t, 8), col), device_id_type=MESH)

    def in_half(copy):
        return B_PIECES[copy[4]][0] // 6 % 2 if copy[1] else A_HALF[copy[4]]

    pl.semaphore_wait(barrier, 22)
    own = [(number, copy) for number, copy in enumerate(COPIES) if copy[0] == 0]
    first = [number for number, copy in own if in_half(copy) == 0]
    @pl.loop(1, 16, unroll=15)
    def _(t):
        meta_a_copy(t).start()

    @pl.loop(1, 8, unroll=7)
    def _(t):
        meta_b_copy(t).start()

    for number in first:
        copy_of(number).start()
    sort_half(1)
    for number, copy in own:
        if in_half(copy) == 1:
            copy_of(number).start()

    for load in loads[4:]:
        load.wait()

    @pl.loop(0, 16)
    def _(o):
        first, last = I32(32), I32(-1)
        for m in range(32):
            here = owners[m] == o
            first = jnp.where(here, jnp.minimum(first, m), first)
            last = jnp.where(here, m, last)
        some, two = last >= 0, last > first
        first = jnp.where(some, first, 0)
        last = jnp.where(two, last, 0)
        owned_m[2 * o] = rem(first, 4) * 8 + div(first, 4)
        owned_m[2 * o + 1] = rem(last, 4) * 8 + div(last, 4)
        owned_f[2 * o] = jnp.where(some, keep[first], 0).astype(F32)
        owned_f[2 * o + 1] = jnp.where(two, keep[last], 0).astype(F32)

    @pl.loop(0, 32)
    def _(m):
        total[m] = jnp.zeros((W, W), F32)

    @pl.loop(1, 16)
    def _(t):
        source = rem(col + t, 16)
        pltpu.make_async_remote_copy(
            src_ref=meta_a.at[source], dst_ref=meta_a.at[source], send_sem=ma_send.at[t], recv_sem=ma_recv.at[source],
            device_id=(row, source), device_id_type=MESH).wait_recv()

    @pl.loop(1, 8)
    def _(t):
        source = rem(row + t, 8)
        pltpu.make_async_remote_copy(
            src_ref=meta_b.at[source], dst_ref=meta_b.at[source], send_sem=mb_send.at[t], recv_sem=mb_recv.at[source],
            device_id=(source, col), device_id_type=MESH).wait_recv()

    def multiply(qa, half, qb, h, s, g, p):
        first = half * 14
        own_rows = [[meta_a[g, half * 16 + kk * 8 + r] for r in range(8)] for kk in range(2)]
        own_cols = [[meta_b[p, 64 + h * 16 + half * 8 + kk * 4 + c] for c in range(4)] for kk in range(2)]
        no_row = [meta_a[g, 32 + half * 2 + kk] for kk in range(2)]
        no_col = [meta_b[p, 96 + h * 4 + half * 2 + kk] for kk in range(2)]
        for kk in range(2):
            at = h * 12 + half * 6 + kk * 3
            for c in range(4):
                low = b_all[qb, at + min(c, 2)]
                high = b_all[qb, at + max(c - 1, 0)]
                dense[kk * W:(kk + 1) * W, c * W:(c + 1) * W] = jnp.where(
                    c == no_col[kk], jnp.zeros_like(low), jnp.where(c < no_col[kk], low, high))
        for r in range(8):
            left, right = [], []
            for kk in range(2):
                low = a_all[qa, first + kk * 7 + min(r, 6)]
                high = a_all[qa, first + kk * 7 + max(r - 1, 0)]
                left.append(jnp.where(r < no_row[kk], low, high))
                cells = []
                for c in range(4):
                    passed = screen[own_rows[kk][r], own_cols[kk][c], half * 2 + kk, s]
                    passed = jnp.where(r == no_row[kk], 0, passed).astype(F32)
                    cells.append(dense[kk * W:(kk + 1) * W, c * W:(c + 1) * W] * passed.astype(BF16))
                right.append(jnp.concatenate(cells, axis=1))
            part = jnp.dot(
                jnp.concatenate(left, axis=1), jnp.concatenate(right, axis=0), preferred_element_type=F32)
            for c in range(4):
                total[c * 8 + r] += part[:, c * W:(c + 1) * W]

    def pair_of(s):
        g, e = (col + s) & 15, (row + s) & 15
        p, h = e & 7, e >> 3
        qa = 4 * (((g >> 2) - y) & 3) + 2 * (((g >> 1) & 1) ^ zl) + ((g & 1) ^ core)
        qb = 2 * (((p >> 1) - x) & 3) + ((p & 1) ^ zh)
        return g, p, h, qa, qb

    def ready_after(n):
        code = TRIGGERS[n]
        half, which, there = code % 2, code // 2 % 16, partners(n)
        if code < 32:
            g = 4 * ((y + which // 4) & 3) + 2 * (zl ^ (which // 2 % 2)) + (core ^ (which % 2))
            s = (g - col) & 15
            _, _, h, _, qb = pair_of(s)
            at = 2 * qb + h
        else:
            p = 2 * ((x + which // 4) & 3) + (zh ^ (which // 2 % 2))
            s = (p + 8 * (which % 2) - row) & 15
            at = pair_of(s)[3]
        both = lax.shift_right_logical(I32(sum(1 << i for i, v in enumerate(there) if v)), at) & 1
        return jnp.where(both == 1, 2 * s + half, -1)

    def receive(n, low, high):
        if high - low > 1:
            middle = (low + high) // 2
            return lax.cond(n < middle, lambda: receive(n, low, middle), lambda: receive(n, middle, high))
        for arrival in GROUPS[low]:
            arrival_of(*ORDER[arrival - 1]).wait_recv()
            for number, copy in enumerate(COPIES):
                if copy[0] == arrival:
                    copy_of(number).start()
        return ready_after(arrival) if partners(arrival) else I32(-1)

    @pl.loop(0, len(GROUPS))
    def _(n):
        code = receive(n, 0, len(GROUPS))

        @pl.when(code >= 0)
        def _():
            s, half = code >> 1, code & 1
            g, p, h, qa, qb = pair_of(s)
            multiply(qa, half, qb, h, s, g, p)

    def owner_at(u):
        dy, dz, dk = rem(2 + 3 * u, 4), 1 - div(u, 8), rem(div(u, 4), 2)
        return 4 * rem(y + dy, 4) + 2 * rem(zl + dz, 2) + rem(core + dk, 2)

    def out_copy(u):
        return pltpu.make_async_remote_copy(
            src_ref=stage.at[u], dst_ref=out.at[col], send_sem=out_send.at[u], recv_sem=out_recv.at[col],
            device_id=(row, owner_at(u)), device_id_type=MESH)

    def own_copy():
        return pltpu.make_async_copy(stage.at[OWN], out.at[col], own_sem)

    @pl.loop(0, 16, unroll=4)
    def _(u):
        o = owner_at(u)
        for slot in range(2):
            stage[u, slot] = (total[owned_m[2 * o + slot]] * owned_f[2 * o + slot]).astype(BF16)

        @pl.when(u != OWN)
        def _():
            out_copy(u).start()

        @pl.when(u == OWN)
        def _():
            own_copy().start()

    @pl.loop(1, 16)
    def _(t):
        meta_a_copy(t).wait_send()

    @pl.loop(1, 8)
    def _(t):
        meta_b_copy(t).wait_send()

    for length in sorted(set(LENGTHS)):
        some = [SENT[number] for number, its in enumerate(LENGTHS) if its == length]

        @pl.loop(min(some), max(some) + 1)
        def _(at, length=length):
            block = a_all.at[0, pl.ds(0, length)]
            pltpu.make_async_remote_copy(
                src_ref=block, dst_ref=block, send_sem=sent.at[at], recv_sem=a_recv.at[0],
                device_id=targets["sib"], device_id_type=MESH).wait_send()

    @pl.loop(0, 16)
    def _(u):
        @pl.when(u != OWN)
        def _():
            out_copy(u).wait_send()
            source = owner_at(u)
            pltpu.make_async_remote_copy(
                src_ref=stage.at[u], dst_ref=out.at[source], send_sem=out_send.at[u], recv_sem=out_recv.at[source],
                device_id=(row, source), device_id_type=MESH).wait_recv()

    own_copy().wait()


def on_device(a_blocks, a_rows, b_blocks, b_cols, screen, keep, owners):
    hbm = pl.BlockSpec(memory_space=pl.ANY)
    dma = pltpu.SemaphoreType.DMA
    out = pl.pallas_call(
        kernel,
        out_shape=jax.ShapeDtypeStruct((16, 2, W, W), BF16),
        in_specs=[hbm] * 7,
        out_specs=hbm,
        scratch_shapes=[
            pltpu.SMEM((4, 7), I32),
            pltpu.SMEM((3, 2, 4), I32),
            pltpu.SMEM((7, 3, 4, 16), I32),
            pltpu.SMEM((32,), I32),
            pltpu.SMEM((32,), I32),
            pltpu.VMEM((4, 7, W, W), BF16),
            pltpu.VMEM((8, 3, W, W), BF16),
            pltpu.VMEM((16, 28, W, W), BF16),
            pltpu.VMEM((8, 24, W, W), BF16),
            pltpu.VMEM((32, W, W), F32),
            pltpu.VMEM((2 * W, 4 * W), BF16),
            pltpu.VMEM((16, 2, W, W), BF16),
            pltpu.SMEM((W,), I32),
            pltpu.SMEM((16, W), I32),
            pltpu.SMEM((8, W), I32),
            pltpu.SMEM((32,), I32),
            pltpu.SMEM((32,), F32),
            dma((16 * len(A_PIECES),)),
            dma((8 * len(B_PIECES),)),
            dma((len(COPIES),)),
            dma((16,)),
            dma((16,)),
            dma((8,)),
            dma((8,)),
            dma((16,)),
            dma((16,)),
            dma,
            dma((7,)),
        ],
        compiler_params=pltpu.CompilerParams(
            collective_id=0, has_side_effects=True, vmem_limit_bytes=60 * 2**20),
        cost_estimate=pl.CostEstimate(flops=8_600_000_000, bytes_accessed=4_000_000, transcendentals=0),
        name="gather_multiply_send",
    )(
        a_blocks[0, 0], b_blocks[0, 0].reshape(8, 3, W, W), a_rows[0, 0], jnp.transpose(b_cols[0, 0], (2, 0, 1)),
        jnp.transpose(screen[0, 0], (2, 3, 1, 0)), keep[0, 0], owners[0, 0, :, 0],
    )
    return out[None, None]


def solution(mesh):
    in_specs = (
        P("row", "col", None, None, None, None),
        P("row", "col", None, None),
        P("row", "col", None, None, None, None, None),
        P("row", "col", None, None, None),
        P("row", "col", None, None, None, None),
        P("row", "col", None),
        P("row", "col", None, None),
    )
    out_specs = P("row", "col", None, None, None, None)
    return jax.shard_map(
        on_device, mesh=mesh, in_specs=in_specs, out_specs=out_specs, check_vma=False
    )
```
